32 devices in a mesh: row: 4 (over y, x), col: 8 (over z, core).
Axes of the slice: x: 2, y: 2, z: 4, core: 2. Of those that a mesh axis runs over, the one named last changes fastest.
Arguments:
- pair: float32 [256, 256, 128], P('row', 'col'), may hold values from -6 to 6
- norm_in_gain: float32 [2, 128], replicated, may hold values from 0.1 to 1.9
- w_proj: bfloat16 [2, 128, 512], replicated, may hold values from -0.5 to 0.5
- w_gate: bfloat16 [2, 128, 128], replicated, may hold values from -0.5 to 0.5
- norm_out_gain: float32 [2, 128], replicated, may hold values from 0.1 to 1.9
- w_out: bfloat16 [2, 128, 128], replicated, may hold values from -0.5 to 0.5
Outputs:
- updated: float32 [256, 256, 128], P('row', 'col')
The draws below stay inside these ranges and needn't reach their ends.
All inputs are finite; a program needn't handle non-finite values.
Results may differ from the reference program's by a relative error of at most 0.0049.
Values may be sent and summed in bfloat16 or wider, within the bound.
No kernel may reach another device: no remote copies, remote signals or barrier semaphores. Data moves between devices by JAX's collectives and lax.ppermute only.
A program may use at most 128 MiB of HBM per device.

```python
import jax
import jax.numpy as jnp
from jax import lax

C = 128
HID = 128
N = 256


def shard_levels(rng, dims, split, smallest, high):
    def one(dim, parts):
        heights = jax.random.uniform(jax.random.fold_in(jax.random.fold_in(rng, 6), dim), (parts,), jnp.float32, smallest / len(split), high / len(split))
        return jnp.repeat(jnp.exp(heights), dims[dim] // parts).reshape((-1,) + (1,) * (len(dims) - dim - 1))

    level = one(*split[0])
    for cut in split[1:]:
        level = level * one(*cut)
    return level


def bell_draw(rng, dims, scale, most, pieces=(), dtype=jnp.bfloat16):
    level = shard_levels(rng, dims, pieces, -0.22, 0.18) if pieces else 1.0
    entries = jax.random.normal(rng, dims, jnp.float32) * scale * level
    return jnp.minimum(jnp.maximum(entries, -most), most).astype(dtype)


def setup_inputs(seed: int = 0) -> dict:
    splits = jax.random.split(jax.random.key(seed), 7)
    return {
        "pair": bell_draw(splits[0], (N, N, C), 1.0, 6.0, ((0, 4), (1, 8)), jnp.float32),
        "norm_in_gain": jnp.clip(1.0 + 0.18 * jax.random.normal(splits[1], (2, C), jnp.float32), 0.1, 1.9),
        "w_proj": bell_draw(splits[2], (2, C, 4 * HID), C ** -0.5, 0.5),
        "w_gate": bell_draw(splits[3], (2, C, C), C ** -0.5, 0.5),
        "norm_out_gain": jnp.clip(1.0 + 0.18 * jax.random.normal(splits[4], (2, HID), jnp.float32), 0.1, 1.9),
        "w_out": bell_draw(splits[5], (2, HID, C), HID ** -0.5, 0.5),
    }


def layer_norm(values, gain):
    center = values - lax.optimization_barrier(jnp.mean(values, axis=-1, keepdims=True))
    spread = lax.optimization_barrier(jnp.mean(center * center, axis=-1, keepdims=True))
    return center * lax.rsqrt(spread + 1e-05) * gain

def branches(pair, gain, w_proj, w_gate):
    first_dim, second_dim, chans = pair.shape
    normed = layer_norm(pair, gain).astype(jnp.bfloat16).reshape(first_dim * second_dim, chans)
    proj = jnp.dot(normed, w_proj, preferred_element_type=jnp.float32)
    hidden = w_proj.shape[1] // 4
    left = (jax.nn.sigmoid(proj[:, :hidden]) * proj[:, hidden:2 * hidden]).astype(jnp.bfloat16)
    right = (jax.nn.sigmoid(proj[:, 2 * hidden:3 * hidden]) * proj[:, 3 * hidden:]).astype(jnp.bfloat16)
    gate = jax.nn.sigmoid(jnp.dot(normed, w_gate, preferred_element_type=jnp.float32))
    shape = (first_dim, second_dim, hidden)
    return (left.reshape(shape), right.reshape(shape), gate.reshape(pair.shape))

def finish(pair, summed, gate, gain, w_out):
    mixed = layer_norm(summed, gain).astype(jnp.bfloat16)
    hidden = summed.shape[-1]
    out = jnp.dot(mixed.reshape(-1, hidden), w_out, preferred_element_type=jnp.float32)
    return pair + gate * out.reshape(pair.shape)

def reference(pair, norm_in_gain, w_proj, w_gate, norm_out_gain, w_out):
    left, right, gate = branches(pair, norm_in_gain[0], w_proj[0], w_gate[0])
    summed = jnp.einsum('ikh,jkh->ijh', left.astype(jnp.float32), right.astype(jnp.float32), precision=lax.Precision.HIGHEST)
    first = finish(pair, summed, gate, norm_out_gain[0], w_out[0])
    left, right, gate = branches(first, norm_in_gain[1], w_proj[1], w_gate[1])
    summed = jnp.einsum('kih,kjh->ijh', left.astype(jnp.float32), right.astype(jnp.float32), precision=lax.Precision.HIGHEST)
    return finish(first, summed, gate, norm_out_gain[1], w_out[1])
```

```python
import functools

import jax
import jax.numpy as jnp
from jax import lax
from jax.experimental import pallas as pl
from jax.experimental.pallas import tpu as pltpu
from jax.sharding import PartitionSpec as P

LANES = 128
BF16 = jnp.bfloat16
F32 = jnp.float32
VMEM_LIMIT = 48 * 1024 * 1024


def sigmoid(x):
    return 0.5 * jnp.tanh(0.5 * x) + 0.5


def norm_rows(x, gain):
    center = x - jnp.mean(x, axis=-1, keepdims=True)
    spread = jnp.mean(center * center, axis=-1, keepdims=True)
    return (center * lax.rsqrt(spread + 1e-05) * gain).astype(BF16)


def load_chunk(ref, s, first, second):
    split = LANES // first
    n1 = second // split
    return jnp.concatenate(
        [ref[pl.ds(l * n1 + s, first, stride=second), :] for l in range(split)], axis=0
    )


def store_chunk(ref, s, first, second, value):
    split = LANES // first
    n1 = second // split
    for l in range(split):
        ref[pl.ds(l * n1 + s, first, stride=second), :] = value[l * first : (l + 1) * first]


def emit_branches(normed, s, n1, w_t, planes):
    hidden = w_t.shape[0] // 4
    proj = lax.dot_general(w_t, normed, (((1,), (1,)), ((), ())), preferred_element_type=F32)
    left = sigmoid(proj[:hidden]) * proj[hidden : 2 * hidden]
    right = sigmoid(proj[2 * hidden : 3 * hidden]) * proj[3 * hidden :]
    for t in range(normed.shape[0] // LANES):
        cols = slice(t * LANES, (t + 1) * LANES)
        planes[pl.ds(s + t, hidden, stride=n1), :] = left[:, cols]
        planes[pl.ds(hidden * n1 + s + t, hidden, stride=n1), :] = right[:, cols]


def pack_branches(planes, send_ref):
    ndev, _, rows, _ = send_ref.shape
    for side in range(2):
        part = planes[side * ndev * rows : (side + 1) * ndev * rows, :].astype(BF16)
        send_ref[:, side] = part.reshape(ndev, rows, LANES)


def project_kernel(u, first, second, pair_ref, gain_ref, w_ref, send_ref, planes):
    n1 = second * first // LANES
    w_t = w_ref[u].T
    gain = gain_ref[u : u + 1, :]
    for s in range(0, n1, 2):
        x = jnp.concatenate([load_chunk(pair_ref, s + t, first, second) for t in range(2)], axis=0)
        emit_branches(norm_rows(x, gain), s, n1, w_t, planes)
    pack_branches(planes, send_ref)


def gate_kernel(u, first, second, ordered, pair_ref, gain_ref, w_ref, gate_ref):
    n1 = second * first // LANES
    gain = gain_ref[u : u + 1, :]
    w = w_ref[u]
    for s in range(0, n1, 2):
        if ordered:
            x = pair_ref[s * LANES : (s + 2) * LANES, :]
        else:
            x = jnp.concatenate([load_chunk(pair_ref, s + t, first, second) for t in range(2)], axis=0)
        gate_ref[s * LANES : (s + 2) * LANES, :] = sigmoid(
            jnp.dot(norm_rows(x, gain), w, preferred_element_type=F32)
        )


def triangle_kernel(contract, rows, cols, first, recv_ref, out_ref, left, right):
    ndev, _, depth, n1, _ = recv_ref.shape
    split = LANES // first
    for h in range(depth):
        for side, dense in ((0, left), (1, right)):
            for c in range(cols):
                for l in range(split):
                    at = (c * split + l) * n1
                    dense[at : at + n1, :] = jnp.concatenate(
                        [
                            recv_ref[r * cols + c, side, h, :, l * first : (l + 1) * first]
                            for r in range(rows)
                        ],
                        axis=1,
                    )
        summed = lax.dot_general(
            right[...], left[...], (((contract,), (contract,)), ((), ())), preferred_element_type=F32
        ).astype(BF16)
        for r in range(rows):
            for c in range(cols):
                out_ref[r * cols + c, h] = jnp.concatenate(
                    [
                        summed[(c * split + l) * n1 : (c * split + l + 1) * n1, r * first : (r + 1) * first]
                        for l in range(split)
                    ],
                    axis=1,
                )


def norm_planes(summed_ref, normal):
    hidden, n1, _ = summed_ref.shape
    x = summed_ref[...].astype(F32)
    center = x - jnp.mean(x, axis=0, keepdims=True)
    spread = jnp.mean(center * center, axis=0, keepdims=True)
    normal[...] = (center * lax.rsqrt(spread + 1e-05)).reshape(hidden * n1, LANES)


def output_chunk(normal, s, n1, gain_cols, w):
    hidden = w.shape[0]
    mixed = jnp.concatenate(
        [(normal[pl.ds(s + t, hidden, stride=n1), :] * gain_cols).astype(BF16) for t in range(2)], axis=1
    )
    return lax.dot_general(mixed, w, (((0,), (0,)), ((), ())), preferred_element_type=F32)


def middle_kernel(
    first, second, pair_ref, summed_ref, gate_ref, out_gain_ref, w_out_ref, gain_ref, w_ref,
    first_ref, send_ref, normal, planes,
):
    n1 = second * first // LANES
    hidden = w_out_ref.shape[1]
    norm_planes(summed_ref, normal)
    gain_cols = jnp.broadcast_to(out_gain_ref[0:1, :], (LANES, hidden)).T
    w_t = w_ref[1].T
    gain = gain_ref[1:2, :]
    for s in range(0, n1, 2):
        out = output_chunk(normal, s, n1, gain_cols, w_out_ref[0])
        z = jnp.concatenate([load_chunk(pair_ref, s + t, first, second) for t in range(2)], axis=0)
        at = slice(s * LANES, (s + 2) * LANES)
        z = z + gate_ref[at, :] * out
        first_ref[at, :] = z
        emit_branches(norm_rows(z, gain), s, n1, w_t, planes)
    pack_branches(planes, send_ref)


def last_kernel(
    first, second, pair_ref, summed_ref, gate_ref, out_gain_ref, w_out_ref, updated_ref, normal
):
    n1 = second * first // LANES
    hidden = w_out_ref.shape[1]
    norm_planes(summed_ref, normal)
    gain_cols = jnp.broadcast_to(out_gain_ref[1:2, :], (LANES, hidden)).T
    for s in range(0, n1, 2):
        out = output_chunk(normal, s, n1, gain_cols, w_out_ref[1])
        at = slice(s * LANES, (s + 2) * LANES)
        z = pair_ref[at, :] + gate_ref[at, :] * out
        for t in range(2):
            store_chunk(updated_ref, s + t, first, second, z[t * LANES : (t + 1) * LANES])


def call(kernel, outs, scratch, flops, *args):
    moved = sum(a.size * a.dtype.itemsize for a in args) + sum(o.size * o.dtype.itemsize for o in outs)
    return pl.pallas_call(
        kernel,
        out_shape=outs if len(outs) > 1 else outs[0],
        in_specs=[pl.BlockSpec(memory_space=pltpu.VMEM)] * len(args),
        out_specs=[pl.BlockSpec(memory_space=pltpu.VMEM)] * len(outs)
        if len(outs) > 1
        else pl.BlockSpec(memory_space=pltpu.VMEM),
        scratch_shapes=scratch,
        compiler_params=pltpu.CompilerParams(vmem_limit_bytes=VMEM_LIMIT),
        cost_estimate=pl.CostEstimate(flops=flops, bytes_accessed=moved, transcendentals=0),
    )(*args)


def body(rows, cols, pair, norm_in_gain, w_proj, w_gate, norm_out_gain, w_out):
    first, second, chans = pair.shape
    hidden = w_out.shape[1]
    ndev = rows * cols
    depth = hidden // ndev
    count = first * second
    n1 = count // LANES
    total = rows * first
    axes = ("row", "col")
    flat = pair.reshape(count, chans)

    send_shape = jax.ShapeDtypeStruct((ndev, 2, depth * n1, LANES), BF16)
    planes = pltpu.VMEM((2 * hidden * n1, LANES), F32)
    normal = pltpu.VMEM((hidden * n1, LANES), F32)
    flat_shape = jax.ShapeDtypeStruct((count, chans), F32)
    proj_flops = 2 * count * chans * 4 * hidden
    gate_flops = 2 * count * chans * chans

    def exchange(block):
        return lax.all_to_all(block, axes, 0, 0, tiled=True)

    def triangle(recv, contract):
        out = call(
            functools.partial(triangle_kernel, contract, rows, cols, first),
            [jax.ShapeDtypeStruct((ndev, depth, n1, LANES), BF16)],
            [pltpu.VMEM((cols * second, total), BF16)] * 2,
            2 * depth * total**3,
            recv.reshape(ndev, 2, depth, n1, LANES),
        )
        return exchange(out).reshape(hidden, n1, LANES)

    send = call(
        functools.partial(project_kernel, 0, first, second),
        [send_shape], [planes], proj_flops, flat, norm_in_gain, w_proj,
    )
    recv = exchange(send)
    gate = call(
        functools.partial(gate_kernel, 0, first, second, False),
        [flat_shape], [], gate_flops, flat, norm_in_gain, w_gate,
    )
    summed = triangle(recv, 0)
    middle, send = call(
        functools.partial(middle_kernel, first, second),
        [flat_shape, send_shape], [normal, planes], proj_flops + gate_flops,
        flat, summed, gate, norm_out_gain, w_out, norm_in_gain, w_proj,
    )
    recv = exchange(send)
    gate = call(
        functools.partial(gate_kernel, 1, first, second, True),
        [flat_shape], [], gate_flops, middle, norm_in_gain, w_gate,
    )
    summed = triangle(recv, 1)
    updated = call(
        functools.partial(last_kernel, first, second),
        [flat_shape], [normal], gate_flops,
        middle, summed, gate, norm_out_gain, w_out,
    )
    return updated.reshape(pair.shape)


def solution(mesh):
    placed = (P("row", "col", None), P(), P(), P(), P(), P())
    return jax.shard_map(
        functools.partial(body, mesh.shape["row"], mesh.shape["col"]),
        mesh=mesh,
        in_specs=placed,
        out_specs=P("row", "col", None),
        check_vma=False,
    )
```

```python
import functools

import jax
import jax.numpy as jnp
from jax import lax
from jax.experimental import pallas as pl
from jax.experimental.pallas import tpu as pltpu
from jax.sharding import PartitionSpec as P

LANES = 128
BF16 = jnp.bfloat16
F32 = jnp.float32
VMEM_LIMIT = 16 * 1024 * 1024
FULL_LIMIT = 63 * 1024 * 1024
PIECES = 2


def sigmoid(x):
    return 0.5 * jnp.tanh(0.5 * x) + 0.5


def norm_rows(x, gain):
    center = x - jnp.mean(x, axis=-1, keepdims=True)
    spread = jnp.mean(center * center, axis=-1, keepdims=True)
    return (center * lax.rsqrt(spread + 1e-05) * gain).astype(BF16)


def load_chunk(ref, s, first, second):
    split = LANES // first
    n1 = second // split
    return jnp.concatenate(
        [ref[pl.ds(l * n1 + s, first, stride=second), :] for l in range(split)], axis=0
    )


def store_chunk(ref, s, first, second, value):
    split = LANES // first
    n1 = second // split
    for l in range(split):
        ref[pl.ds(l * n1 + s, first, stride=second), :] = value[l * first : (l + 1) * first]


def emit_branches(normed, s, n1, w_t, planes):
    hidden = w_t.shape[0] // 4
    proj = lax.dot_general(w_t, normed, (((1,), (1,)), ((), ())), preferred_element_type=F32)
    left = sigmoid(proj[:hidden]) * proj[hidden : 2 * hidden]
    right = sigmoid(proj[2 * hidden : 3 * hidden]) * proj[3 * hidden :]
    for t in range(normed.shape[0] // LANES):
        cols = slice(t * LANES, (t + 1) * LANES)
        planes[pl.ds(s + t, hidden, stride=n1), :] = left[:, cols]
        planes[pl.ds(hidden * n1 + s + t, hidden, stride=n1), :] = right[:, cols]


def pack_branches(planes, send_ref):
    ndev, _, rows, _ = send_ref.shape
    for side in range(2):
        part = planes[side * ndev * rows : (side + 1) * ndev * rows, :].astype(BF16)
        send_ref[:, side] = part.reshape(ndev, rows, LANES)


def parts_of(hbm, vmem, sems):
    first, second, _ = hbm.shape
    n1 = second * first // LANES
    split = second // n1
    return [
        [
            (hbm.at[:, pl.ds(l * n1 + g * 8, 8), :], vmem.at[:, pl.ds(l * n1 + g * 8, 8), :], sems.at[g * split + l])
            for l in range(split)
        ]
        for g in range(n1 // 8)
    ]


def project_kernel(
    u, pair_hbm, gain_hbm, w_hbm, send_hbm, pair_ref, gain_ref, w_ref, normed, planes, send_ref, sems, in_sems, out_sems
):
    first, second, chans = pair_hbm.shape
    ndev, _, rows, _ = send_ref.shape
    n1 = second * first // LANES
    flat = pair_ref.reshape(first * second, chans)
    small = [
        pltpu.make_async_copy(gain_hbm, gain_ref, sems.at[0]),
        pltpu.make_async_copy(w_hbm.at[u], w_ref, sems.at[1]),
    ]
    parts = [[pltpu.make_async_copy(*c) for c in part] for part in parts_of(pair_hbm, pair_ref, in_sems)]
    for copy in parts[0] + small + [c for part in parts[1:] for c in part]:
        copy.start()
    for copy in small:
        copy.wait()
    w_t = w_ref[...].T
    hidden = w_t.shape[0] // 4
    gain = gain_ref[u : u + 1, :]
    pieces = out_sems.shape[0]
    height, owners = hidden // pieces, ndev // pieces
    sent = []
    for piece in range(pieces):
        w_piece = jnp.concatenate(
            [w_t[k * hidden + piece * height : k * hidden + (piece + 1) * height] for k in range(4)], axis=0
        )
        for s in range(0, n1, 2):
            at = slice(s * LANES, (s + 2) * LANES)
            if piece == 0:
                if s % 8 == 0:
                    for copy in parts[s // 8]:
                        copy.wait()
                x = jnp.concatenate([load_chunk(flat, s + t, first, second) for t in range(2)], axis=0)
                y = norm_rows(x, gain)
                normed[at, :] = y
            else:
                y = normed[at, :]
            emit_branches(y, s, n1, w_piece, planes.at[piece])
        own = pl.ds(piece * owners, owners)
        pack_branches(planes.at[piece], send_ref.at[own])
        sent.append(pltpu.make_async_copy(send_ref.at[own], send_hbm.at[own], out_sems.at[piece]))
        sent[-1].start()
    for copy in sent:
        copy.wait()


def gate_kernel(u, first, second, ordered, pair_ref, gain_ref, w_ref, gate_ref):
    n1 = second * first // LANES
    gain = gain_ref[u : u + 1, :]
    w = w_ref[u]
    for s in range(0, n1, 2):
        if ordered:
            x = pair_ref[s * LANES : (s + 2) * LANES, :]
        else:
            x = jnp.concatenate([load_chunk(pair_ref, s + t, first, second) for t in range(2)], axis=0)
        gate_ref[s * LANES : (s + 2) * LANES, :] = sigmoid(
            jnp.dot(norm_rows(x, gain), w, preferred_element_type=F32)
        )


def triangle_kernel(contract, rows, cols, first, recv_ref, out_ref, left, right):
    ndev, _, depth, n1, _ = recv_ref.shape
    split = LANES // first
    for h in range(depth):
        for side, dense in ((0, left), (1, right)):
            for c in range(cols):
                for l in range(split):
                    at = (c * split + l) * n1
                    dense[at : at + n1, :] = jnp.concatenate(
                        [
                            recv_ref[r * cols + c, side, h, :, l * first : (l + 1) * first]
                            for r in range(rows)
                        ],
                        axis=1,
                    )
        summed = lax.dot_general(
            right[...], left[...], (((contract,), (contract,)), ((), ())), preferred_element_type=F32
        ).astype(BF16)
        for r in range(rows):
            for c in range(cols):
                out_ref[r * cols + c, h] = jnp.concatenate(
                    [
                        summed[(c * split + l) * n1 : (c * split + l + 1) * n1, r * first : (r + 1) * first]
                        for l in range(split)
                    ],
                    axis=1,
                )


def norm_planes(summed_ref, normal):
    hidden, n1, _ = summed_ref.shape
    x = summed_ref[...].astype(F32)
    center = x - jnp.mean(x, axis=0, keepdims=True)
    spread = jnp.mean(center * center, axis=0, keepdims=True)
    normal[...] = (center * lax.rsqrt(spread + 1e-05)).reshape(hidden * n1, LANES)


def output_chunk(normal, s, n1, gain_cols, w):
    hidden = w.shape[0]
    mixed = jnp.concatenate(
        [(normal[pl.ds(s + t, hidden, stride=n1), :] * gain_cols).astype(BF16) for t in range(2)], axis=1
    )
    return lax.dot_general(mixed, w, (((0,), (0,)), ((), ())), preferred_element_type=F32)


def middle_kernel(
    first, second, pair_ref, summed_ref, gate_ref, out_gain_ref, w_out_ref, gain_ref, w_ref,
    first_ref, send_ref, normal, planes,
):
    n1 = second * first // LANES
    hidden = w_out_ref.shape[1]
    norm_planes(summed_ref, normal)
    gain_cols = jnp.broadcast_to(out_gain_ref[0:1, :], (LANES, hidden)).T
    w_t = w_ref[1].T
    gain = gain_ref[1:2, :]
    for s in range(0, n1, 2):
        out = output_chunk(normal, s, n1, gain_cols, w_out_ref[0])
        z = jnp.concatenate([load_chunk(pair_ref, s + t, first, second) for t in range(2)], axis=0)
        at = slice(s * LANES, (s + 2) * LANES)
        z = z + gate_ref[at, :] * out
        first_ref[at, :] = z
        emit_branches(norm_rows(z, gain), s, n1, w_t, planes)
    pack_branches(planes, send_ref)


def last_kernel(
    pair_ref, summed_ref, gate_ref, out_gain_ref, w_out_ref, updated_hbm, normal, updated_ref, sems
):
    first, second, chans = updated_hbm.shape
    n1 = second * first // LANES
    hidden = w_out_ref.shape[1]
    flat = updated_ref.reshape(first * second, chans)
    parts = [
        [pltpu.make_async_copy(vmem, hbm, sem) for hbm, vmem, sem in part]
        for part in parts_of(updated_hbm, updated_ref, sems)
    ]
    norm_planes(summed_ref, normal)
    gain_cols = jnp.broadcast_to(out_gain_ref[1:2, :], (LANES, hidden)).T
    for s in range(0, n1, 2):
        out = output_chunk(normal, s, n1, gain_cols, w_out_ref[1])
        at = slice(s * LANES, (s + 2) * LANES)
        z = pair_ref[at, :] + gate_ref[at, :] * out
        for t in range(2):
            store_chunk(flat, s + t, first, second, z[t * LANES : (t + 1) * LANES])
        if s % 8 == 6:
            for copy in parts[s // 8]:
                copy.start()
    for part in parts:
        for copy in part:
            copy.wait()


def call(kernel, outs, scratch, flops, *args, ins=pltpu.VMEM, spaces=None, limit=VMEM_LIMIT):
    moved = sum(a.size * a.dtype.itemsize for a in args) + sum(o.size * o.dtype.itemsize for o in outs)
    out_specs = [pl.BlockSpec(memory_space=space) for space in spaces or [pltpu.VMEM] * len(outs)]
    several = len(outs) > 1
    return pl.pallas_call(
        kernel,
        out_shape=outs if several else outs[0],
        in_specs=[pl.BlockSpec(memory_space=ins)] * len(args),
        out_specs=out_specs if several else out_specs[0],
        scratch_shapes=scratch,
        compiler_params=pltpu.CompilerParams(vmem_limit_bytes=limit),
        cost_estimate=pl.CostEstimate(flops=flops, bytes_accessed=moved, transcendentals=0),
    )(*args)


def body(rows, cols, pair, norm_in_gain, w_proj, w_gate, norm_out_gain, w_out):
    first, second, chans = pair.shape
    hidden = w_out.shape[1]
    ndev = rows * cols
    depth = hidden // ndev
    count = first * second
    n1 = count // LANES
    total = rows * first
    axes = ("row", "col")
    flat = pair.reshape(count, chans)

    send_shape = jax.ShapeDtypeStruct((ndev, 2, depth * n1, LANES), BF16)
    planes = pltpu.VMEM((2 * hidden * n1, LANES), F32)
    normal = pltpu.VMEM((hidden * n1, LANES), F32)
    flat_shape = jax.ShapeDtypeStruct((count, chans), F32)
    proj_flops = 2 * count * chans * 4 * hidden
    gate_flops = 2 * count * chans * chans

    def exchange(block):
        return lax.all_to_all(block, axes, 0, 0, tiled=True)

    def triangle(recv, contract):
        out = call(
            functools.partial(triangle_kernel, contract, rows, cols, first),
            [jax.ShapeDtypeStruct((ndev, depth, n1, LANES), BF16)],
            [pltpu.VMEM((cols * second, total), BF16)] * 2,
            2 * depth * total**3,
            recv.reshape(ndev, 2, depth, n1, LANES),
        )
        return exchange(out).reshape(hidden, n1, LANES)

    slabs = pltpu.SemaphoreType.DMA((second // 8,))
    staged = [
        pltpu.VMEM(pair.shape, F32),
        pltpu.VMEM(norm_in_gain.shape, F32),
        pltpu.VMEM(w_proj.shape[1:], BF16),
        pltpu.VMEM((count, chans), BF16),
        pltpu.VMEM((PIECES, 2 * hidden * n1 // PIECES, LANES), F32),
        pltpu.VMEM(send_shape.shape, BF16),
        pltpu.SemaphoreType.DMA((2,)),
        slabs,
        pltpu.SemaphoreType.DMA((PIECES,)),
    ]
    send = call(
        functools.partial(project_kernel, 0),
        [send_shape], staged, proj_flops, pair, norm_in_gain, w_proj,
        ins=pltpu.HBM, spaces=[pltpu.HBM], limit=FULL_LIMIT,
    )
    recv = exchange(send)
    gate = call(
        functools.partial(gate_kernel, 0, first, second, False),
        [flat_shape], [], gate_flops, flat, norm_in_gain, w_gate,
    )
    recv, gate = lax.optimization_barrier((recv, gate))
    summed = triangle(recv, 0)
    middle, send = call(
        functools.partial(middle_kernel, first, second),
        [flat_shape, send_shape],
        [normal, planes],
        proj_flops + gate_flops,
        flat, summed, gate, norm_out_gain, w_out, norm_in_gain, w_proj,
    )
    recv = exchange(send)
    gate = call(
        functools.partial(gate_kernel, 1, first, second, True),
        [flat_shape], [], gate_flops, middle, norm_in_gain, w_gate,
    )
    recv, gate = lax.optimization_barrier((recv, gate))
    summed = triangle(recv, 1)
    return call(
        last_kernel,
        [jax.ShapeDtypeStruct(pair.shape, F32)], [normal, pltpu.VMEM(pair.shape, F32), slabs], gate_flops,
        middle, summed, gate, norm_out_gain, w_out, spaces=[pltpu.HBM],
    )


def solution(mesh):
    placed = (P("row", "col", None), P(), P(), P(), P(), P())
    return jax.shard_map(
        functools.partial(body, mesh.shape["row"], mesh.shape["col"]),
        mesh=mesh,
        in_specs=placed,
        out_specs=P("row", "col", None),
        check_vma=False,
    )
```

```python
import functools

import jax
import jax.numpy as jnp
from jax import lax
from jax.experimental import pallas as pl
from jax.experimental.pallas import tpu as pltpu
from jax.sharding import PartitionSpec as P

LANES = 128
BF16 = jnp.bfloat16
F32 = jnp.float32
VMEM_LIMIT = 16 * 1024 * 1024
FULL_LIMIT = 63 * 1024 * 1024


def sigmoid(x):
    return 0.5 * jnp.tanh(0.5 * x) + 0.5


def norm_rows(x, gain):
    center = x - jnp.mean(x, axis=-1, keepdims=True)
    spread = jnp.mean(center * center, axis=-1, keepdims=True)
    return (center * lax.rsqrt(spread + 1e-05) * gain).astype(BF16)


def block_rows(first, second):
    split = LANES // first
    n1 = second // split
    return [l * n1 + s for s in range(n1) for l in range(split)]


def load_block(padded, first, second):
    rows = block_rows(first, second)
    return jnp.concatenate([padded[pl.ds(row, first, stride=second + 1), :] for row in rows], axis=0)


def block_copies(hbm, padded, sems):
    first, second, _ = hbm.shape
    return [(hbm.at[f], padded.at[pl.ds(f * (second + 1), second), :], sems.at[f]) for f in range(first)]


def emit_branches(normed, w_t, planes, send_ref, done=None):
    ndev, _, rows, _ = send_ref.shape
    hidden = w_t.shape[0] // 4
    depth = hidden // ndev
    n1 = rows // depth
    pad = n1 + 1
    proj = lax.dot_general(w_t, normed, (((1,), (1,)), ((), ())), preferred_element_type=F32)
    for side in range(2):
        at = 2 * side * hidden
        value = sigmoid(proj[at : at + hidden]) * proj[at + hidden : at + 2 * hidden]
        for s in range(n1):
            planes[pl.ds(side * hidden * pad + s, hidden, stride=pad), :] = value[:, s * LANES : (s + 1) * LANES]
    for device in range(ndev):
        for side in range(2):
            for h in range(depth):
                at = (side * hidden + device * depth + h) * pad
                send_ref[device, side, h * n1 : (h + 1) * n1, :] = planes[at : at + n1, :].astype(BF16)
        if done is not None:
            done(device)


def project_kernel(
    u, pair_hbm, gain_hbm, w_hbm, send_hbm, padded, gain_ref, w_ref, planes, send_ref, in_sems, out_sems
):
    first, second, _ = pair_hbm.shape
    ndev = send_ref.shape[0]
    copies = [pltpu.make_async_copy(*c) for c in block_copies(pair_hbm, padded, in_sems)]
    copies.append(pltpu.make_async_copy(gain_hbm, gain_ref, in_sems.at[first]))
    copies.append(pltpu.make_async_copy(w_hbm.at[u], w_ref, in_sems.at[first + 1]))
    for copy in copies:
        copy.start()
    for copy in copies:
        copy.wait()
    half = ndev // 2
    sent = []

    def send(device):
        if (device + 1) % half == 0:
            own = pl.ds(device + 1 - half, half)
            copy = pltpu.make_async_copy(send_ref.at[own], send_hbm.at[own], out_sems.at[len(sent)])
            copy.start()
            sent.append(copy)

    normed = norm_rows(load_block(padded, first, second), gain_ref[u : u + 1, :])
    emit_branches(normed, w_ref[...].T, planes, send_ref, send)
    for copy in sent:
        copy.wait()


def prepare_kernel(
    pair_ref, gain_ref, w_gate_ref, w_ref, out_gain_ref,
    ordered_ref, gate_ref, w_t_ref, gain_cols_ref, padded,
):
    first, second, _ = pair_ref.shape
    for f in range(first):
        padded[f * (second + 1) : f * (second + 1) + second, :] = pair_ref[f]
    x = load_block(padded, first, second)
    ordered_ref[...] = x
    normed = norm_rows(x, gain_ref[0:1, :])
    gate_ref[...] = sigmoid(jnp.dot(normed, w_gate_ref[0], preferred_element_type=F32))
    w_t_ref[...] = w_ref[1].T
    for u in range(2):
        wide = (LANES, out_gain_ref.shape[1])
        gain_cols_ref[u] = jnp.broadcast_to(out_gain_ref[u : u + 1, :], wide).T


def triangle_kernel(contract, rows, cols, first, recv_ref, out_ref, left, right):
    ndev, _, depth, n1, _ = recv_ref.shape
    split = LANES // first
    for h in range(depth):
        for side, dense in ((0, left), (1, right)):
            for c in range(cols):
                for l in range(split):
                    at = (c * split + l) * n1
                    dense[at : at + n1, :] = jnp.concatenate(
                        [
                            recv_ref[r * cols + c, side, h, :, l * first : (l + 1) * first]
                            for r in range(rows)
                        ],
                        axis=1,
                    )
        summed = lax.dot_general(
            right[...], left[...], (((contract,), (contract,)), ((), ())), preferred_element_type=F32
        ).astype(BF16)
        for r in range(rows):
            for c in range(cols):
                out_ref[r * cols + c, h] = jnp.concatenate(
                    [
                        summed[(c * split + l) * n1 : (c * split + l + 1) * n1, r * first : (r + 1) * first]
                        for l in range(split)
                    ],
                    axis=1,
                )


def output(summed_ref, gain_cols, w, normal):
    hidden, n1, _ = summed_ref.shape
    pad = n1 + 1
    x = summed_ref[...].astype(F32)
    center = x - jnp.mean(x, axis=0, keepdims=True)
    spread = jnp.mean(center * center, axis=0, keepdims=True)
    scaled = center * lax.rsqrt(spread + 1e-05)
    for h in range(hidden):
        normal[h * pad : h * pad + n1, :] = scaled[h]
    mixed = jnp.concatenate(
        [(normal[pl.ds(s, hidden, stride=pad), :] * gain_cols).astype(BF16) for s in range(n1)], axis=1
    )
    return lax.dot_general(mixed, w, (((0,), (0,)), ((), ())), preferred_element_type=F32)


def middle_kernel(
    ordered_ref, summed_ref, gate_ref, gain_cols_ref, w_out_ref, gain_ref, w_t_ref, w_gate_ref,
    first_ref, gate_out_ref, send_ref, normal, planes,
):
    z = ordered_ref[...] + gate_ref[...] * output(summed_ref, gain_cols_ref[0], w_out_ref[0], normal)
    first_ref[...] = z
    normed = norm_rows(z, gain_ref[1:2, :])
    emit_branches(normed, w_t_ref[...], planes, send_ref)
    gate_out_ref[...] = sigmoid(jnp.dot(normed, w_gate_ref[1], preferred_element_type=F32))


def last_kernel(
    first_ref, summed_ref, gate_ref, gain_cols_ref, w_out_ref, updated_hbm, normal, padded, sems
):
    first, second, _ = updated_hbm.shape
    z = first_ref[...] + gate_ref[...] * output(summed_ref, gain_cols_ref[1], w_out_ref[1], normal)
    for i, row in enumerate(block_rows(first, second)):
        padded[pl.ds(row, first, stride=second + 1), :] = z[i * first : (i + 1) * first]
    copies = [
        pltpu.make_async_copy(vmem, hbm, sem) for hbm, vmem, sem in block_copies(updated_hbm, padded, sems)
    ]
    for copy in copies:
        copy.start()
    for copy in copies:
        copy.wait()


def call(kernel, outs, scratch, flops, *args, ins=pltpu.VMEM, spaces=None, limit=VMEM_LIMIT):
    moved = sum(a.size * a.dtype.itemsize for a in args) + sum(o.size * o.dtype.itemsize for o in outs)
    out_specs = [pl.BlockSpec(memory_space=space) for space in spaces or [pltpu.VMEM] * len(outs)]
    several = len(outs) > 1
    return pl.pallas_call(
        kernel,
        out_shape=outs if several else outs[0],
        in_specs=[pl.BlockSpec(memory_space=ins)] * len(args),
        out_specs=out_specs if several else out_specs[0],
        scratch_shapes=scratch,
        compiler_params=pltpu.CompilerParams(vmem_limit_bytes=limit),
        cost_estimate=pl.CostEstimate(flops=flops, bytes_accessed=moved, transcendentals=0),
    )(*args)


def body(rows, cols, pair, norm_in_gain, w_proj, w_gate, norm_out_gain, w_out):
    first, second, chans = pair.shape
    hidden = w_out.shape[1]
    ndev = rows * cols
    depth = hidden // ndev
    count = first * second
    n1 = count // LANES
    total = rows * first
    axes = ("row", "col")

    send_shape = jax.ShapeDtypeStruct((ndev, 2, depth * n1, LANES), BF16)
    flat_shape = jax.ShapeDtypeStruct((count, chans), F32)
    planes = pltpu.VMEM((2 * hidden * (n1 + 1), LANES), F32)
    normal = pltpu.VMEM((hidden * (n1 + 1), LANES), F32)
    padded = pltpu.VMEM((first * (second + 1), chans), F32)
    proj_flops = 2 * count * chans * 4 * hidden
    gate_flops = 2 * count * chans * chans

    def exchange(block):
        return lax.all_to_all(block, axes, 0, 0, tiled=True)

    def triangle(recv, contract):
        out = call(
            functools.partial(triangle_kernel, contract, rows, cols, first),
            [jax.ShapeDtypeStruct((ndev, depth, n1, LANES), BF16)],
            [pltpu.VMEM((cols * second, total), BF16)] * 2,
            2 * depth * total**3,
            recv.reshape(ndev, 2, depth, n1, LANES),
        )
        return exchange(out).reshape(hidden, n1, LANES)

    send = call(
        functools.partial(project_kernel, 0),
        [send_shape],
        [
            padded,
            pltpu.VMEM(norm_in_gain.shape, F32),
            pltpu.VMEM(w_proj.shape[1:], BF16),
            planes,
            pltpu.VMEM(send_shape.shape, BF16),
            pltpu.SemaphoreType.DMA((first + 2,)),
            pltpu.SemaphoreType.DMA((2,)),
        ],
        proj_flops, pair, norm_in_gain, w_proj,
        ins=pltpu.HBM, spaces=[pltpu.HBM], limit=FULL_LIMIT,
    )
    recv = exchange(send)
    prepared = call(
        prepare_kernel,
        [
            flat_shape,
            flat_shape,
            jax.ShapeDtypeStruct((4 * hidden, chans), BF16),
            jax.ShapeDtypeStruct((2, hidden, LANES), F32),
        ],
        [padded], gate_flops,
        pair, norm_in_gain, w_gate, w_proj, norm_out_gain,
    )
    recv, (ordered, gate, w_t, gain_cols) = lax.optimization_barrier((recv, prepared))
    summed = triangle(recv, 0)
    middle, gate, send = call(
        middle_kernel,
        [flat_shape, flat_shape, send_shape], [normal, planes], proj_flops + 2 * gate_flops,
        ordered, summed, gate, gain_cols, w_out, norm_in_gain, w_t, w_gate,
    )
    summed = triangle(exchange(send), 1)
    return call(
        last_kernel,
        [jax.ShapeDtypeStruct(pair.shape, F32)], [normal, padded, pltpu.SemaphoreType.DMA((first,))], gate_flops,
        middle, summed, gate, gain_cols, w_out, spaces=[pltpu.HBM],
    )


def solution(mesh):
    placed = (P("row", "col", None), P(), P(), P(), P(), P())
    return jax.shard_map(
        functools.partial(body, mesh.shape["row"], mesh.shape["col"]),
        mesh=mesh,
        in_specs=placed,
        out_specs=P("row", "col", None),
        check_vma=False,
    )
```

```python
import functools

import jax
import jax.numpy as jnp
from jax import lax
from jax.experimental import pallas as pl
from jax.experimental.pallas import tpu as pltpu
from jax.sharding import PartitionSpec as P

LANES = 128
BF16 = jnp.bfloat16
F32 = jnp.float32
VMEM_LIMIT = 16 * 1024 * 1024
FULL_LIMIT = 63 * 1024 * 1024


def sigmoid(x):
    return 0.5 * jnp.tanh(0.5 * x) + 0.5


def norm_rows(x, gain):
    center = x - jnp.mean(x, axis=-1, keepdims=True)
    spread = jnp.mean(center * center, axis=-1, keepdims=True)
    return (center * lax.rsqrt(spread + 1e-05) * gain).astype(BF16)


def block_rows(first, second):
    split = LANES // first
    n1 = second // split
    return [l * n1 + s for s in range(n1) for l in range(split)]


def load_block(padded, first, second):
    rows = block_rows(first, second)
    return jnp.concatenate([padded[pl.ds(row, first, stride=second + 1), :] for row in rows], axis=0)


def block_copies(hbm, padded, sem):
    first, second, _ = hbm.shape
    return [(hbm.at[f], padded.at[pl.ds(f * (second + 1), second), :], sem) for f in range(first)]


def wait_block(hbm, padded, sem):
    first, second, chans = hbm.shape
    whole = padded.at[pl.ds(0, first * second), :]
    pltpu.make_async_copy(whole, whole, sem).wait()


def emit_branches(normed, w_t, planes, send_ref, done=None):
    ndev, _, rows, _ = send_ref.shape
    hidden = w_t.shape[0] // 4
    depth = hidden // ndev
    n1 = rows // depth
    pad = n1 + 1
    proj = lax.dot_general(w_t, normed, (((1,), (1,)), ((), ())), preferred_element_type=F32)
    for side in range(2):
        at = 2 * side * hidden
        value = sigmoid(proj[at : at + hidden]) * proj[at + hidden : at + 2 * hidden]
        for s in range(n1):
            planes[pl.ds(side * hidden * pad + s, hidden, stride=pad), :] = value[:, s * LANES : (s + 1) * LANES]
    for device in range(ndev):
        for side in range(2):
            for h in range(depth):
                at = (side * hidden + device * depth + h) * pad
                send_ref[device, side, h * n1 : (h + 1) * n1, :] = planes[at : at + n1, :].astype(BF16)
        if done is not None:
            done(device)


def project_kernel(
    u, pair_hbm, gain_hbm, w_hbm, send_hbm, padded, gain_ref, w_ref, planes, send_ref, in_sems, out_sems
):
    first, second, _ = pair_hbm.shape
    ndev = send_ref.shape[0]
    copies = [pltpu.make_async_copy(*c) for c in block_copies(pair_hbm, padded, in_sems.at[0])]
    small = [
        pltpu.make_async_copy(gain_hbm, gain_ref, in_sems.at[1]),
        pltpu.make_async_copy(w_hbm.at[u], w_ref, in_sems.at[2]),
    ]
    for copy in small + copies:
        copy.start()
    for copy in small:
        copy.wait()
    wait_block(pair_hbm, padded, in_sems.at[0])
    half = ndev // 2
    sent = []

    def send(device):
        if (device + 1) % half == 0:
            own = pl.ds(device + 1 - half, half)
            copy = pltpu.make_async_copy(send_ref.at[own], send_hbm.at[own], out_sems.at[len(sent)])
            copy.start()
            sent.append(copy)

    normed = norm_rows(load_block(padded, first, second), gain_ref[u : u + 1, :])
    emit_branches(normed, w_ref[...].T, planes, send_ref, send)
    for copy in sent:
        copy.wait()


def prepare_kernel(
    pair_ref, gain_ref, w_gate_ref, w_ref, out_gain_ref,
    ordered_ref, gate_ref, w_t_ref, gain_cols_ref, padded,
):
    first, second, _ = pair_ref.shape
    for f in range(first):
        padded[f * (second + 1) : f * (second + 1) + second, :] = pair_ref[f]
    x = load_block(padded, first, second)
    ordered_ref[...] = x
    normed = norm_rows(x, gain_ref[0:1, :])
    gate_ref[...] = sigmoid(jnp.dot(normed, w_gate_ref[0], preferred_element_type=F32))
    w_t_ref[...] = w_ref[1].T
    for u in range(2):
        wide = (LANES, out_gain_ref.shape[1])
        gain_cols_ref[u] = jnp.broadcast_to(out_gain_ref[u : u + 1, :], wide).T


def triangle_kernel(contract, rows, cols, first, recv_ref, out_ref, left, right):
    ndev, _, depth, n1, _ = recv_ref.shape
    split = LANES // first
    for h in range(depth):
        for side, dense in ((0, left), (1, right)):
            for c in range(cols):
                for l in range(split):
                    at = (c * split + l) * n1
                    dense[at : at + n1, :] = jnp.concatenate(
                        [
                            recv_ref[r * cols + c, side, h, :, l * first : (l + 1) * first]
                            for r in range(rows)
                        ],
                        axis=1,
                    )
        summed = lax.dot_general(
            right[...], left[...], (((contract,), (contract,)), ((), ())), preferred_element_type=F32
        ).astype(BF16)
        for r in range(rows):
            for c in range(cols):
                out_ref[r * cols + c, h] = jnp.concatenate(
                    [
                        summed[(c * split + l) * n1 : (c * split + l + 1) * n1, r * first : (r + 1) * first]
                        for l in range(split)
                    ],
                    axis=1,
                )


def output(summed_ref, gain_cols, w, normal):
    hidden, n1, _ = summed_ref.shape
    pad = n1 + 1
    x = summed_ref[...].astype(F32)
    center = x - jnp.mean(x, axis=0, keepdims=True)
    spread = jnp.mean(center * center, axis=0, keepdims=True)
    scaled = center * lax.rsqrt(spread + 1e-05)
    for h in range(hidden):
        normal[h * pad : h * pad + n1, :] = scaled[h]
    mixed = jnp.concatenate(
        [(normal[pl.ds(s, hidden, stride=pad), :] * gain_cols).astype(BF16) for s in range(n1)], axis=1
    )
    return lax.dot_general(mixed, w, (((0,), (0,)), ((), ())), preferred_element_type=F32)


def middle_kernel(
    ordered_ref, summed_ref, gate_ref, gain_cols_ref, w_out_ref, gain_ref, w_t_ref, w_gate_ref,
    first_ref, gate_out_ref, send_ref, normal, planes,
):
    z = ordered_ref[...] + gate_ref[...] * output(summed_ref, gain_cols_ref[0], w_out_ref[0], normal)
    first_ref[...] = z
    normed = norm_rows(z, gain_ref[1:2, :])
    emit_branches(normed, w_t_ref[...], planes, send_ref)
    gate_out_ref[...] = sigmoid(jnp.dot(normed, w_gate_ref[1], preferred_element_type=F32))


def last_kernel(
    first_ref, summed_ref, gate_ref, gain_cols_ref, w_out_ref, updated_hbm, normal, padded, sems
):
    first, second, _ = updated_hbm.shape
    z = first_ref[...] + gate_ref[...] * output(summed_ref, gain_cols_ref[1], w_out_ref[1], normal)
    for i, row in enumerate(block_rows(first, second)):
        padded[pl.ds(row, first, stride=second + 1), :] = z[i * first : (i + 1) * first]
    copies = [
        pltpu.make_async_copy(vmem, hbm, sem) for hbm, vmem, sem in block_copies(updated_hbm, padded, sems.at[0])
    ]
    for copy in copies:
        copy.start()
    wait_block(updated_hbm, padded, sems.at[0])


def call(kernel, outs, scratch, flops, *args, ins=pltpu.VMEM, spaces=None, limit=VMEM_LIMIT):
    moved = sum(a.size * a.dtype.itemsize for a in args) + sum(o.size * o.dtype.itemsize for o in outs)
    out_specs = [pl.BlockSpec(memory_space=space) for space in spaces or [pltpu.VMEM] * len(outs)]
    several = len(outs) > 1
    return pl.pallas_call(
        kernel,
        out_shape=outs if several else outs[0],
        in_specs=[pl.BlockSpec(memory_space=ins)] * len(args),
        out_specs=out_specs if several else out_specs[0],
        scratch_shapes=scratch,
        compiler_params=pltpu.CompilerParams(vmem_limit_bytes=limit),
        cost_estimate=pl.CostEstimate(flops=flops, bytes_accessed=moved, transcendentals=0),
    )(*args)


def body(rows, cols, pair, norm_in_gain, w_proj, w_gate, norm_out_gain, w_out):
    first, second, chans = pair.shape
    hidden = w_out.shape[1]
    ndev = rows * cols
    depth = hidden // ndev
    count = first * second
    n1 = count // LANES
    total = rows * first
    axes = ("row", "col")

    send_shape = jax.ShapeDtypeStruct((ndev, 2, depth * n1, LANES), BF16)
    flat_shape = jax.ShapeDtypeStruct((count, chans), F32)
    planes = pltpu.VMEM((2 * hidden * (n1 + 1), LANES), F32)
    normal = pltpu.VMEM((hidden * (n1 + 1), LANES), F32)
    padded = pltpu.VMEM((first * (second + 1), chans), F32)
    proj_flops = 2 * count * chans * 4 * hidden
    gate_flops = 2 * count * chans * chans

    def exchange(block):
        return lax.all_to_all(block, axes, 0, 0, tiled=True)

    def triangle(recv, contract):
        out = call(
            functools.partial(triangle_kernel, contract, rows, cols, first),
            [jax.ShapeDtypeStruct((ndev, depth, n1, LANES), BF16)],
            [pltpu.VMEM((cols * second, total), BF16)] * 2,
            2 * depth * total**3,
            recv.reshape(ndev, 2, depth, n1, LANES),
        )
        return exchange(out).reshape(hidden, n1, LANES)

    send = call(
        functools.partial(project_kernel, 0),
        [send_shape],
        [
            padded,
            pltpu.VMEM(norm_in_gain.shape, F32),
            pltpu.VMEM(w_proj.shape[1:], BF16),
            planes,
            pltpu.VMEM(send_shape.shape, BF16),
            pltpu.SemaphoreType.DMA((3,)),
            pltpu.SemaphoreType.DMA((2,)),
        ],
        proj_flops, pair, norm_in_gain, w_proj,
        ins=pltpu.HBM, spaces=[pltpu.HBM], limit=FULL_LIMIT,
    )
    recv = exchange(send)
    prepared = call(
        prepare_kernel,
        [
            flat_shape,
            flat_shape,
            jax.ShapeDtypeStruct((4 * hidden, chans), BF16),
            jax.ShapeDtypeStruct((2, hidden, LANES), F32),
        ],
        [padded], gate_flops,
        pair, norm_in_gain, w_gate, w_proj, norm_out_gain,
    )
    recv, (ordered, gate, w_t, gain_cols) = lax.optimization_barrier((recv, prepared))
    summed = triangle(recv, 0)
    middle, gate, send = call(
        middle_kernel,
        [flat_shape, flat_shape, send_shape], [normal, planes], proj_flops + 2 * gate_flops,
        ordered, summed, gate, gain_cols, w_out, norm_in_gain, w_t, w_gate,
    )
    summed = triangle(exchange(send), 1)
    return call(
        last_kernel,
        [jax.ShapeDtypeStruct(pair.shape, F32)], [normal, padded, pltpu.SemaphoreType.DMA((1,))], gate_flops,
        middle, summed, gate, gain_cols, w_out, spaces=[pltpu.HBM],
    )


def solution(mesh):
    placed = (P("row", "col", None), P(), P(), P(), P(), P())
    return jax.shard_map(
        functools.partial(body, mesh.shape["row"], mesh.shape["col"]),
        mesh=mesh,
        in_specs=placed,
        out_specs=P("row", "col", None),
        check_vma=False,
    )
```

```python
import functools

import jax
import jax.numpy as jnp
from jax import lax
from jax.experimental import pallas as pl
from jax.experimental.pallas import tpu as pltpu
from jax.sharding import PartitionSpec as P

LANES = 128
BF16 = jnp.bfloat16
F32 = jnp.float32
VMEM_LIMIT = 16 * 1024 * 1024


def sigmoid(x):
    return 0.5 * jnp.tanh(0.5 * x) + 0.5


def norm_rows(x, gain):
    center = x - jnp.mean(x, axis=-1, keepdims=True)
    spread = jnp.mean(center * center, axis=-1, keepdims=True)
    return (center * lax.rsqrt(spread + 1e-05) * gain).astype(BF16)


def block_rows(first, second):
    split = LANES // first
    n1 = second // split
    return [l * n1 + s for s in range(n1) for l in range(split)]


def load_block(padded, first, second):
    rows = block_rows(first, second)
    return jnp.concatenate([padded[pl.ds(row, first, stride=second + 1), :] for row in rows], axis=0)


def block_copies(hbm, padded, sem):
    first, second, _ = hbm.shape
    return [(hbm.at[f], padded.at[pl.ds(f * (second + 1), second), :], sem) for f in range(first)]


def wait_block(hbm, padded, sem):
    first, second, chans = hbm.shape
    whole = padded.at[pl.ds(0, first * second), :]
    pltpu.make_async_copy(whole, whole, sem).wait()


def branch_planes(normed, w_t, n1, planes):
    hidden = w_t.shape[0] // 4
    pad = n1 + 1
    proj = lax.dot_general(w_t, normed, (((1,), (1,)), ((), ())), preferred_element_type=F32)
    for side in range(2):
        at = 2 * side * hidden
        value = sigmoid(proj[at : at + hidden]) * proj[at + hidden : at + 2 * hidden]
        for s in range(n1):
            planes[pl.ds(side * hidden * pad + s, hidden, stride=pad), :] = value[:, s * LANES : (s + 1) * LANES]


def plane(planes, n1, channel):
    at = channel * (n1 + 1)
    return planes[at : at + n1, :].astype(BF16)


def project_kernel(
    u, pair_hbm, gain_hbm, w_hbm, send_hbm, padded, gain_ref, w_ref, planes, send_ref, in_sems, out_sems
):
    first, second, _ = pair_hbm.shape
    ndev = send_ref.shape[0]
    copies = [pltpu.make_async_copy(*c) for c in block_copies(pair_hbm, padded, in_sems.at[0])]
    small = [
        pltpu.make_async_copy(gain_hbm, gain_ref, in_sems.at[1]),
        pltpu.make_async_copy(w_hbm.at[u], w_ref, in_sems.at[2]),
    ]
    for copy in small + copies:
        copy.start()
    for copy in small:
        copy.wait()
    wait_block(pair_hbm, padded, in_sems.at[0])
    depth, n1 = send_ref.shape[2:4]
    hidden = ndev * depth
    normed = norm_rows(load_block(padded, first, second), gain_ref[u : u + 1, :])
    branch_planes(normed, w_ref[...].T, n1, planes)
    sent = []
    for part in range(2):
        own = range(part * ndev // 2, (part + 1) * ndev // 2)
        for device in own:
            for side in range(2):
                for h in range(depth):
                    send_ref[device, side, h] = plane(planes, n1, side * hidden + device * depth + h)
        at = pl.ds(own[0], len(own))
        sent.append(pltpu.make_async_copy(send_ref.at[at], send_hbm.at[at], out_sems.at[part]))
        sent[-1].start()
    for copy in sent:
        copy.wait()


def move(copies):
    for copy in copies:
        copy.start()
    for copy in copies:
        copy.wait()


def prepare_kernel(
    pair_hbm, gain_ref, w_gate_ref, w_ref, out_gain_ref,
    ordered_hbm, gate_hbm, w_t_ref, gain_cols_ref, padded, ordered_ref, gate_ref, sems,
):
    first, second, _ = pair_hbm.shape
    for copy in block_copies(pair_hbm, padded, sems.at[0]):
        pltpu.make_async_copy(*copy).start()
    w_t_ref[...] = w_ref[1].T
    for u in range(2):
        wide = (LANES, out_gain_ref.shape[1])
        gain_cols_ref[u] = jnp.broadcast_to(out_gain_ref[u : u + 1, :], wide).T
    wait_block(pair_hbm, padded, sems.at[0])
    x = load_block(padded, first, second)
    ordered_ref[...] = x
    normed = norm_rows(x, gain_ref[0:1, :])
    gate_ref[...] = sigmoid(jnp.dot(normed, w_gate_ref[0], preferred_element_type=F32))
    move([
        pltpu.make_async_copy(ordered_ref, ordered_hbm, sems.at[1]),
        pltpu.make_async_copy(gate_ref, gate_hbm, sems.at[2]),
    ])


def gate_kernel(first_hbm, gain_ref, w_gate_ref, gate_hbm, first_ref, gate_ref, sems):
    move([pltpu.make_async_copy(first_hbm, first_ref, sems.at[0])])
    normed = norm_rows(first_ref[...], gain_ref[1:2, :])
    gate_ref[...] = sigmoid(jnp.dot(normed, w_gate_ref[1], preferred_element_type=F32))
    move([pltpu.make_async_copy(gate_ref, gate_hbm, sems.at[1])])


def outgoing_kernel(cols, first, recv_ref, out_ref, left, right):
    ndev, _, depth, n1, _ = recv_ref.shape
    split = LANES // first
    rows = ndev // cols
    for h in range(depth):
        for side, dense in ((0, left), (1, right)):
            for c in range(cols):
                for l in range(split):
                    at = (c * split + l) * n1
                    dense[at : at + n1, :] = jnp.concatenate(
                        [
                            recv_ref[r * cols + c, side, h, :, l * first : (l + 1) * first]
                            for r in range(rows)
                        ],
                        axis=1,
                    )
        summed = lax.dot_general(
            right[...], left[...], (((0,), (0,)), ((), ())), preferred_element_type=F32
        ).astype(BF16)
        scatter_product(summed, rows, cols, first, h, out_ref)


def scatter_product(summed, rows, cols, first, h, out_ref):
    split = LANES // first
    n1 = out_ref.shape[2]
    for r in range(rows):
        for c in range(cols):
            out_ref[r * cols + c, h] = jnp.concatenate(
                [
                    summed[(c * split + l) * n1 : (c * split + l + 1) * n1, r * first : (r + 1) * first]
                    for l in range(split)
                ],
                axis=1,
            )


def incoming_kernel(cols, first, recv_ref, *refs):
    *part_refs, out_ref, left, right, b_ref = refs
    ndev, depth, n1, _ = recv_ref.shape
    split = LANES // first
    rows = ndev // cols
    for r in range(rows):
        b_ref[0, r] = part_refs[r][...]
    for apart, part_ref in enumerate(part_refs[rows:], 1):
        b_ref[apart] = part_ref[...]
    my_row, my_rest = lax.axis_index("row"), lax.axis_index("rest")
    for h in range(depth):
        for c in range(cols):
            for l in range(split):
                at = (c * split + l) * n1
                left[at : at + n1, :] = jnp.concatenate(
                    [recv_ref[r * cols + c, h, :, l * first : (l + 1) * first] for r in range(rows)], axis=1
                )
        for c in range(cols // 2):
            apart = jnp.bitwise_xor(my_rest, c)
            for l in range(split):
                at = (c * split + l) * n1
                right[at : at + n1, :] = jnp.concatenate(
                    [
                        b_ref[apart // 2, jnp.bitwise_xor(my_row, r), apart % 2, h, :, l * first : (l + 1) * first]
                        for r in range(rows)
                    ],
                    axis=1,
                )
        summed = lax.dot_general(
            right[...], left[...], (((1,), (1,)), ((), ())), preferred_element_type=F32
        ).astype(BF16)
        scatter_product(summed, rows, cols // 2, first, h, out_ref)


def output(summed_ref, gain_cols, w, normal):
    hidden, n1, _ = summed_ref.shape
    pad = n1 + 1
    x = summed_ref[...].astype(F32)
    center = x - jnp.mean(x, axis=0, keepdims=True)
    spread = jnp.mean(center * center, axis=0, keepdims=True)
    scaled = center * lax.rsqrt(spread + 1e-05)
    for h in range(hidden):
        normal[h * pad : h * pad + n1, :] = scaled[h]
    mixed = jnp.concatenate(
        [(normal[pl.ds(s, hidden, stride=pad), :] * gain_cols).astype(BF16) for s in range(n1)], axis=1
    )
    return lax.dot_general(mixed, w, (((0,), (0,)), ((), ())), preferred_element_type=F32)


def middle_kernel(
    ordered_ref, summed_ref, gate_ref, gain_cols_ref, w_out_ref, gain_ref, w_t_ref,
    first_hbm, send_hbm, keep_hbm, swap_hbm, normal, planes, first_ref, send_ref, b_ref, sems,
):
    rows, halves, rest, depth, n1, _ = send_ref.shape
    hidden = rows * rest * depth
    copies = []

    def leave(vmem, hbm):
        copies.append(pltpu.make_async_copy(vmem, hbm, sems.at[len(copies)]))
        copies[-1].start()

    z = ordered_ref[...] + gate_ref[...] * output(summed_ref, gain_cols_ref[0], w_out_ref[0], normal)
    first_ref[...] = z
    leave(first_ref, first_hbm)
    branch_planes(norm_rows(z, gain_ref[1:2, :]), w_t_ref[...], n1, planes)
    my_row, my_rest = lax.axis_index("row"), lax.axis_index("rest")
    for r in range(rows):
        for c in range(rest):
            apart = jnp.bitwise_xor(my_rest, c)
            at = (r * rest + c) * depth
            for h in range(depth):
                b_ref[apart % 2, jnp.bitwise_xor(my_row, r), apart // 2, h] = plane(planes, n1, hidden + at + h)
    leave(b_ref.at[1], swap_hbm)
    leave(b_ref.at[0], keep_hbm)
    for r in range(rows):
        for c in range(rest):
            at = (r * rest + c) * depth
            for h in range(depth):
                value = plane(planes, n1, at + h)
                for half in range(halves):
                    send_ref[r, half, c, h] = value
        if r % (rows // 2) == rows // 2 - 1:
            own = pl.ds(r + 1 - rows // 2, rows // 2)
            leave(send_ref.at[own], send_hbm.at[own])
    for copy in copies:
        copy.wait()


def last_kernel(
    first_ref, summed_ref, gate_ref, gain_cols_ref, w_out_ref, updated_hbm, normal, padded, sems
):
    first, second, _ = updated_hbm.shape
    z = first_ref[...] + gate_ref[...] * output(summed_ref, gain_cols_ref[1], w_out_ref[1], normal)
    for i, row in enumerate(block_rows(first, second)):
        padded[pl.ds(row, first, stride=second + 1), :] = z[i * first : (i + 1) * first]
    copies = [
        pltpu.make_async_copy(vmem, hbm, sem) for hbm, vmem, sem in block_copies(updated_hbm, padded, sems.at[0])
    ]
    for copy in copies:
        copy.start()
    wait_block(updated_hbm, padded, sems.at[0])


def call(kernel, outs, scratch, flops, *args, pinned=None, spaces=None):
    moved = sum(a.size * a.dtype.itemsize for a in args) + sum(o.size * o.dtype.itemsize for o in outs)
    pinned = pinned or [None] * len(args)
    spaces = spaces or [None] * len(outs)
    args = [a if space is None else pltpu.with_memory_space_constraint(a, space) for a, space in zip(args, pinned)]
    outs = [o if space is None else space(o.shape, o.dtype) for o, space in zip(outs, spaces)]
    in_specs = [pl.BlockSpec(memory_space=space or pltpu.VMEM) for space in pinned]
    out_specs = [pl.BlockSpec(memory_space=space or pltpu.VMEM) for space in spaces]
    several = len(outs) > 1
    return pl.pallas_call(
        kernel,
        out_shape=outs if several else outs[0],
        in_specs=in_specs,
        out_specs=out_specs if several else out_specs[0],
        scratch_shapes=scratch,
        compiler_params=pltpu.CompilerParams(vmem_limit_bytes=VMEM_LIMIT),
        cost_estimate=pl.CostEstimate(flops=flops, bytes_accessed=moved, transcendentals=0),
    )(*args)


def spread(keep, swap):
    rows, highs = keep.shape[:2]
    rest = 2 * highs

    def swapped(x, axis, size, apart):
        return lax.ppermute(x, axis, [(d, d ^ apart) for d in range(size)]) if apart else x

    b = jnp.stack([keep, swapped(swap, "rest", rest, 1)], axis=2)
    far = [
        swapped(jnp.stack([swapped(b[r, c], "row", rows, r) for r in range(rows)]), "rest", rest, 2 * c)
        for c in range(1, highs)
    ]
    return [swapped(b[r, 0], "row", rows, r) for r in range(rows)] + far


def body(rows, cols, pair, norm_in_gain, w_proj, w_gate, norm_out_gain, w_out):
    first, second, chans = pair.shape
    hidden = w_out.shape[1]
    ndev = rows * cols
    rest = cols // 2
    depth, half_depth = hidden // ndev, 2 * hidden // ndev
    count = first * second
    n1 = count // LANES
    total = rows * first

    flat_shape = jax.ShapeDtypeStruct((count, chans), F32)
    planes = pltpu.VMEM((2 * hidden * (n1 + 1), LANES), F32)
    normal = pltpu.VMEM((hidden * (n1 + 1), LANES), F32)
    padded = pltpu.VMEM((first * (second + 1), chans), F32)
    proj_flops = 2 * count * chans * 4 * hidden
    gate_flops = 2 * count * chans * chans
    tri_flops = 2 * depth * total**3

    def shaped(*shape):
        return jax.ShapeDtypeStruct(shape + (n1, LANES), BF16)

    send = call(
        functools.partial(project_kernel, 0),
        [shaped(ndev, 2, depth)],
        [
            padded,
            pltpu.VMEM(norm_in_gain.shape, F32),
            pltpu.VMEM(w_proj.shape[1:], BF16),
            planes,
            pltpu.VMEM((ndev, 2, depth, n1, LANES), BF16),
            pltpu.SemaphoreType.DMA((3,)),
            pltpu.SemaphoreType.DMA((2,)),
        ],
        proj_flops, pair, norm_in_gain, w_proj,
        pinned=[pltpu.HBM] * 3, spaces=[pltpu.HBM],
    )
    recv = lax.all_to_all(send, ("row", "half", "rest"), 0, 0, tiled=True)
    prepared = call(
        prepare_kernel,
        [
            flat_shape,
            flat_shape,
            jax.ShapeDtypeStruct((4 * hidden, chans), BF16),
            jax.ShapeDtypeStruct((2, hidden, LANES), F32),
        ],
        [padded, pltpu.VMEM(flat_shape.shape, F32), pltpu.VMEM(flat_shape.shape, F32), pltpu.SemaphoreType.DMA((3,))],
        gate_flops,
        pair, norm_in_gain, w_gate, w_proj, norm_out_gain,
        pinned=[pltpu.HBM] + [None] * 4, spaces=[pltpu.HBM, pltpu.HBM, None, None],
    )
    recv, (ordered, gate, w_t, gain_cols) = lax.optimization_barrier((recv, prepared))
    product = call(
        functools.partial(outgoing_kernel, cols, first),
        [shaped(ndev, depth)], [pltpu.VMEM((cols * second, total), BF16)] * 2, tri_flops, recv,
    )
    summed = lax.all_to_all(product, ("row", "half", "rest"), 0, 0, tiled=True)
    send_shape, b_shape = shaped(rows, 2, rest, half_depth), shaped(rows, rest // 2, half_depth)
    middle, send, keep, swap = call(
        middle_kernel,
        [flat_shape, send_shape, b_shape, b_shape],
        [
            normal,
            planes,
            pltpu.VMEM(flat_shape.shape, F32),
            pltpu.VMEM(send_shape.shape, BF16),
            pltpu.VMEM((2,) + b_shape.shape, BF16),
            pltpu.SemaphoreType.DMA((5,)),
        ],
        proj_flops + gate_flops,
        ordered, summed.reshape(hidden, n1, LANES), gate, gain_cols, w_out, norm_in_gain, w_t,
        spaces=[pltpu.HBM] * 4,
    )
    recv = lax.all_to_all(
        send.reshape(ndev, half_depth, n1, LANES), ("row", "half", "rest"), 0, 0, tiled=True
    )
    gate = call(
        gate_kernel, [flat_shape],
        [pltpu.VMEM(flat_shape.shape, F32), pltpu.VMEM(flat_shape.shape, F32), pltpu.SemaphoreType.DMA((2,))],
        gate_flops, middle, norm_in_gain, w_gate,
        pinned=[pltpu.HBM, None, None], spaces=[pltpu.HBM],
    )
    recv, gate = lax.optimization_barrier((recv, gate))
    product = call(
        functools.partial(incoming_kernel, cols, first),
        [shaped(rows * rest, half_depth)],
        [
            pltpu.VMEM((cols * second, total), BF16),
            pltpu.VMEM((rest * second, total), BF16),
            pltpu.VMEM((rest // 2, rows, 2, half_depth, n1, LANES), BF16),
        ],
        tri_flops, recv, *spread(keep, swap),
    )
    summed = lax.all_to_all(product, ("row", "rest"), 0, 0, tiled=True)
    return call(
        last_kernel,
        [jax.ShapeDtypeStruct(pair.shape, F32)], [normal, padded, pltpu.SemaphoreType.DMA((1,))], gate_flops,
        middle, summed.reshape(hidden, n1, LANES), gate, gain_cols, w_out, spaces=[pltpu.HBM],
    )


def solution(mesh):
    rows, cols = mesh.shape["row"], mesh.shape["col"]
    halved = jax.sharding.Mesh(mesh.devices.reshape(rows, 2, cols // 2), ("row", "half", "rest"))
    block = P("row", ("half", "rest"), None)
    return jax.shard_map(
        functools.partial(body, rows, cols),
        mesh=halved,
        in_specs=(block, P(), P(), P(), P(), P()),
        out_specs=block,
        check_vma=False,
    )
```

```python
import functools

import jax
import jax.numpy as jnp
from jax import lax
from jax.experimental import pallas as pl
from jax.experimental.pallas import tpu as pltpu
from jax.sharding import PartitionSpec as P

LANES = 128
BF16 = jnp.bfloat16
F32 = jnp.float32
VMEM_LIMIT = 16 * 1024 * 1024


def sigmoid(x):
    return 0.5 * jnp.tanh(0.5 * x) + 0.5


def norm_rows(x, gain):
    center = x - jnp.mean(x, axis=-1, keepdims=True)
    spread = jnp.mean(center * center, axis=-1, keepdims=True)
    return (center * lax.rsqrt(spread + 1e-05) * gain).astype(BF16)


def block_rows(first, second):
    split = LANES // first
    n1 = second // split
    return [l * n1 + s for s in range(n1) for l in range(split)]


def load_block(padded, first, second):
    rows = block_rows(first, second)
    return jnp.concatenate([padded[pl.ds(row, first, stride=second + 1), :] for row in rows], axis=0)


def block_copies(hbm, padded, sem):
    first, second, _ = hbm.shape
    return [(hbm.at[f], padded.at[pl.ds(f * (second + 1), second), :], sem) for f in range(first)]


def wait_block(hbm, padded, sem):
    first, second, chans = hbm.shape
    whole = padded.at[pl.ds(0, first * second), :]
    pltpu.make_async_copy(whole, whole, sem).wait()


def branch_planes(normed, w_t, n1, planes):
    hidden = w_t.shape[0] // 4
    pad = n1 + 1
    proj = lax.dot_general(w_t, normed, (((1,), (1,)), ((), ())), preferred_element_type=F32)
    for side in range(2):
        at = 2 * side * hidden
        value = sigmoid(proj[at : at + hidden]) * proj[at + hidden : at + 2 * hidden]
        for s in range(n1):
            planes[pl.ds(side * hidden * pad + s, hidden, stride=pad), :] = value[:, s * LANES : (s + 1) * LANES]


def plane(planes, n1, channel):
    at = channel * (n1 + 1)
    return planes[at : at + n1, :].astype(BF16)


def relative_blocks(b_ref, planes, n1, channels):
    rows, highs = b_ref.shape[1:3]
    my_row, my_rest = lax.axis_index("row"), lax.axis_index("rest")
    for r in range(rows):
        for c in range(2 * highs):
            apart = jnp.bitwise_xor(my_rest, c)
            for i, channel in enumerate(channels(r, c)):
                b_ref[apart % 2, jnp.bitwise_xor(my_row, r), apart // 2, i] = plane(planes, n1, channel)


def project_kernel(shared, pair_hbm, gain_hbm, w_hbm, send_hbm, *refs):
    if shared:
        keep_hbm, swap_hbm, padded, gain_ref, w_ref, planes, send_ref, b_ref, in_sems, out_sems = refs
    else:
        padded, gain_ref, w_ref, planes, send_ref, in_sems, out_sems = refs
    first, second, _ = pair_hbm.shape
    ndev, _, depth, n1, _ = send_ref.shape
    hidden = ndev * (depth + shared)
    copies = [pltpu.make_async_copy(*c) for c in block_copies(pair_hbm, padded, in_sems.at[0])]
    small = [
        pltpu.make_async_copy(gain_hbm, gain_ref, in_sems.at[1]),
        pltpu.make_async_copy(w_hbm.at[0], w_ref, in_sems.at[2]),
    ]
    for copy in small + copies:
        copy.start()
    for copy in small:
        copy.wait()
    wait_block(pair_hbm, padded, in_sems.at[0])
    normed = norm_rows(load_block(padded, first, second), gain_ref[0:1, :])
    branch_planes(normed, w_ref[...].T, n1, planes)
    sent = []

    def leave(vmem, hbm):
        sent.append(pltpu.make_async_copy(vmem, hbm, out_sems.at[len(sent)]))
        sent[-1].start()

    if shared:
        rest = 2 * b_ref.shape[2]

        def channels(r, c):
            at = ndev * depth + (r * rest + c) * 2 * shared
            return [side * hidden + at + h for side in range(2) for h in range(2 * shared)]

        relative_blocks(b_ref, planes, n1, channels)
        leave(b_ref.at[1], swap_hbm)
        leave(b_ref.at[0], keep_hbm)
    for part in range(2):
        own = range(part * ndev // 2, (part + 1) * ndev // 2)
        for device in own:
            for side in range(2):
                for h in range(depth):
                    send_ref[device, side, h] = plane(planes, n1, side * hidden + device * depth + h)
        at = pl.ds(own[0], len(own))
        leave(send_ref.at[at], send_hbm.at[at])
    for copy in sent:
        copy.wait()


def move(copies):
    for copy in copies:
        copy.start()
    for copy in copies:
        copy.wait()


def prepare_kernel(
    pair_hbm, gain_ref, w_gate_ref, w_ref, out_gain_ref,
    ordered_hbm, gate_hbm, w_t_ref, gain_cols_ref, padded, ordered_ref, gate_ref, sems,
):
    first, second, _ = pair_hbm.shape
    for copy in block_copies(pair_hbm, padded, sems.at[0]):
        pltpu.make_async_copy(*copy).start()
    w_t_ref[...] = w_ref[1].T
    for u in range(2):
        wide = (LANES, out_gain_ref.shape[1])
        gain_cols_ref[u] = jnp.broadcast_to(out_gain_ref[u : u + 1, :], wide).T
    wait_block(pair_hbm, padded, sems.at[0])
    x = load_block(padded, first, second)
    ordered_ref[...] = x
    normed = norm_rows(x, gain_ref[0:1, :])
    gate_ref[...] = sigmoid(jnp.dot(normed, w_gate_ref[0], preferred_element_type=F32))
    move([
        pltpu.make_async_copy(ordered_ref, ordered_hbm, sems.at[1]),
        pltpu.make_async_copy(gate_ref, gate_hbm, sems.at[2]),
    ])


def gate_kernel(first_hbm, gain_ref, w_gate_ref, gate_hbm, first_ref, gate_ref, sems):
    move([pltpu.make_async_copy(first_hbm, first_ref, sems.at[0])])
    normed = norm_rows(first_ref[...], gain_ref[1:2, :])
    gate_ref[...] = sigmoid(jnp.dot(normed, w_gate_ref[1], preferred_element_type=F32))
    move([pltpu.make_async_copy(gate_ref, gate_hbm, sems.at[1])])


def stage(part_refs, b_ref):
    rows = b_ref.shape[1]
    for r in range(rows):
        b_ref[0, r] = part_refs[r][...]
    for apart, part_ref in enumerate(part_refs[rows:], 1):
        b_ref[apart] = part_ref[...]


def dense_half(b_ref, i, first, dense):
    highs, rows, _, _, n1, _ = b_ref.shape
    split = LANES // first
    my_row, my_rest = lax.axis_index("row"), lax.axis_index("rest")
    for c in range(2 * highs):
        apart = jnp.bitwise_xor(my_rest, c)
        for l in range(split):
            at = (c * split + l) * n1
            dense[at : at + n1, :] = jnp.concatenate(
                [
                    b_ref[apart // 2, jnp.bitwise_xor(my_row, r), apart % 2, i, :, l * first : (l + 1) * first]
                    for r in range(rows)
                ],
                axis=1,
            )


def outgoing_kernel(cols, first, shared, recv_ref, *refs):
    if shared:
        *part_refs, out_ref, left, right, half_left, half_right, b_ref = refs
    else:
        out_ref, left, right = refs
    ndev, _, depth, n1, _ = recv_ref.shape
    split = LANES // first
    rows = ndev // cols

    def product(left, right):
        return lax.dot_general(
            right[...], left[...], (((0,), (0,)), ((), ())), preferred_element_type=F32
        ).astype(BF16)

    for h in range(depth):
        for side, dense in ((0, left), (1, right)):
            for c in range(cols):
                for l in range(split):
                    at = (c * split + l) * n1
                    dense[at : at + n1, :] = jnp.concatenate(
                        [
                            recv_ref[r * cols + c, side, h, :, l * first : (l + 1) * first]
                            for r in range(rows)
                        ],
                        axis=1,
                    )
        scatter_product(product(left, right), rows, cols, first, h, out_ref)
    if shared:
        stage(part_refs, b_ref)
        for h in range(2 * shared):
            dense_half(b_ref, h, first, half_left)
            dense_half(b_ref, 2 * shared + h, first, half_right)
            scatter_product(product(half_left, half_right), rows, cols, first, depth + h, out_ref)


def scatter_product(summed, rows, cols, first, h, out_ref):
    split = LANES // first
    n1 = out_ref.shape[2]
    for r in range(rows):
        for c in range(cols):
            out_ref[r * cols + c, h] = jnp.concatenate(
                [
                    summed[(c * split + l) * n1 : (c * split + l + 1) * n1, r * first : (r + 1) * first]
                    for l in range(split)
                ],
                axis=1,
            )


def incoming_kernel(cols, first, recv_ref, *refs):
    *part_refs, out_ref, left, right, b_ref = refs
    ndev, depth, n1, _ = recv_ref.shape
    split = LANES // first
    rows = ndev // cols
    stage(part_refs, b_ref)
    for h in range(depth):
        for c in range(cols):
            for l in range(split):
                at = (c * split + l) * n1
                left[at : at + n1, :] = jnp.concatenate(
                    [recv_ref[r * cols + c, h, :, l * first : (l + 1) * first] for r in range(rows)], axis=1
                )
        dense_half(b_ref, h, first, right)
        summed = lax.dot_general(
            right[...], left[...], (((1,), (1,)), ((), ())), preferred_element_type=F32
        ).astype(BF16)
        scatter_product(summed, rows, cols // 2, first, h, out_ref)


def output(x, gain_cols, w, normal):
    hidden, n1, _ = x.shape
    pad = n1 + 1
    center = x - jnp.mean(x, axis=0, keepdims=True)
    spread = jnp.mean(center * center, axis=0, keepdims=True)
    scaled = center * lax.rsqrt(spread + 1e-05)
    for h in range(hidden):
        normal[h * pad : h * pad + n1, :] = scaled[h]
    mixed = jnp.concatenate(
        [(normal[pl.ds(s, hidden, stride=pad), :] * gain_cols).astype(BF16) for s in range(n1)], axis=1
    )
    return lax.dot_general(mixed, w, (((0,), (0,)), ((), ())), preferred_element_type=F32)


def middle_kernel(
    ordered_ref, summed_ref, gate_ref, gain_cols_ref, w_out_ref, gain_ref, w_t_ref,
    first_hbm, send_hbm, keep_hbm, swap_hbm, normal, planes, first_ref, send_ref, b_ref, sems,
):
    rows, halves, rest, depth, n1, _ = send_ref.shape
    hidden = rows * rest * depth
    copies = []

    def leave(vmem, hbm):
        copies.append(pltpu.make_async_copy(vmem, hbm, sems.at[len(copies)]))
        copies[-1].start()

    shared = summed_ref.shape[3] - depth // 2
    own = summed_ref.shape[3] - 2 * shared
    x = summed_ref[:, :, :, :own].astype(F32).reshape(-1, n1, LANES)
    if shared:
        x_shared = summed_ref[:, 0, :, own:].astype(F32) + summed_ref[:, 1, :, own:].astype(F32)
        x = jnp.concatenate([x, x_shared.reshape(-1, n1, LANES)], axis=0)
    z = ordered_ref[...] + gate_ref[...] * output(x, gain_cols_ref[0], w_out_ref[0], normal)
    first_ref[...] = z
    leave(first_ref, first_hbm)
    branch_planes(norm_rows(z, gain_ref[1:2, :]), w_t_ref[...], n1, planes)
    relative_blocks(
        b_ref, planes, n1, lambda r, c: [hidden + (r * rest + c) * depth + h for h in range(depth)]
    )
    leave(b_ref.at[1], swap_hbm)
    leave(b_ref.at[0], keep_hbm)
    for r in range(rows):
        for c in range(rest):
            at = (r * rest + c) * depth
            for h in range(depth):
                value = plane(planes, n1, at + h)
                for half in range(halves):
                    send_ref[r, half, c, h] = value
        if r % (rows // 2) == rows // 2 - 1:
            own = pl.ds(r + 1 - rows // 2, rows // 2)
            leave(send_ref.at[own], send_hbm.at[own])
    for copy in copies:
        copy.wait()


def last_kernel(
    first_ref, summed_ref, gate_ref, gain_cols_ref, w_out_ref, updated_hbm, normal, padded, sems
):
    first, second, _ = updated_hbm.shape
    z = first_ref[...] + gate_ref[...] * output(summed_ref[...].astype(F32), gain_cols_ref[1], w_out_ref[1], normal)
    for i, row in enumerate(block_rows(first, second)):
        padded[pl.ds(row, first, stride=second + 1), :] = z[i * first : (i + 1) * first]
    copies = [
        pltpu.make_async_copy(vmem, hbm, sem) for hbm, vmem, sem in block_copies(updated_hbm, padded, sems.at[0])
    ]
    for copy in copies:
        copy.start()
    wait_block(updated_hbm, padded, sems.at[0])


def call(kernel, outs, scratch, flops, *args, pinned=None, spaces=None):
    moved = sum(a.size * a.dtype.itemsize for a in args) + sum(o.size * o.dtype.itemsize for o in outs)
    pinned = pinned or [None] * len(args)
    spaces = spaces or [None] * len(outs)
    args = [a if space is None else pltpu.with_memory_space_constraint(a, space) for a, space in zip(args, pinned)]
    outs = [o if space is None else space(o.shape, o.dtype) for o, space in zip(outs, spaces)]
    in_specs = [pl.BlockSpec(memory_space=space or pltpu.VMEM) for space in pinned]
    out_specs = [pl.BlockSpec(memory_space=space or pltpu.VMEM) for space in spaces]
    return pl.pallas_call(
        kernel,
        out_shape=outs,
        in_specs=in_specs,
        out_specs=out_specs,
        scratch_shapes=scratch,
        compiler_params=pltpu.CompilerParams(vmem_limit_bytes=VMEM_LIMIT),
        cost_estimate=pl.CostEstimate(flops=flops, bytes_accessed=moved, transcendentals=0),
    )(*args)


def spread(keep, swap):
    rows, highs = keep.shape[:2]
    rest = 2 * highs

    def swapped(x, axis, size, apart):
        return lax.ppermute(x, axis, [(d, d ^ apart) for d in range(size)]) if apart else x

    b = jnp.stack([keep, swapped(swap, "rest", rest, 1)], axis=2)
    far = [
        swapped(jnp.stack([swapped(b[r, c], "row", rows, r) for r in range(rows)]), "rest", rest, 2 * c)
        for c in range(1, highs)
    ]
    return [swapped(b[r, 0], "row", rows, r) for r in range(rows)] + far


def body(rows, cols, pair, norm_in_gain, w_proj, w_gate, norm_out_gain, w_out):
    first, second, chans = pair.shape
    hidden = w_out.shape[1]
    ndev = rows * cols
    rest = cols // 2
    shared = hidden // ndev // 4
    depth, half_depth = hidden // ndev - shared, 2 * hidden // ndev
    count = first * second
    n1 = count // LANES
    total = rows * first

    flat_shape = jax.ShapeDtypeStruct((count, chans), F32)
    planes = pltpu.VMEM((2 * hidden * (n1 + 1), LANES), F32)
    normal = pltpu.VMEM((hidden * (n1 + 1), LANES), F32)
    padded = pltpu.VMEM((first * (second + 1), chans), F32)
    proj_flops = 2 * count * chans * 4 * hidden
    gate_flops = 2 * count * chans * chans
    tri_flops = 2 * (depth + shared) * total**3

    def shaped(*shape):
        return jax.ShapeDtypeStruct(shape + (n1, LANES), BF16)

    out_shapes = [shaped(ndev, 2, depth)] + [shaped(rows, rest // 2, 4 * shared)] * (2 if shared else 0)
    send, *swaps = call(
        functools.partial(project_kernel, shared),
        out_shapes,
        [
            padded,
            pltpu.VMEM(norm_in_gain.shape, F32),
            pltpu.VMEM(w_proj.shape[1:], BF16),
            planes,
            pltpu.VMEM(out_shapes[0].shape, BF16),
        ]
        + ([pltpu.VMEM((2,) + out_shapes[1].shape, BF16)] if shared else [])
        + [pltpu.SemaphoreType.DMA((3,)), pltpu.SemaphoreType.DMA((4,))],
        proj_flops, pair, norm_in_gain, w_proj,
        pinned=[pltpu.HBM] * 3, spaces=[pltpu.HBM] * len(out_shapes),
    )
    recv = lax.all_to_all(send, ("row", "half", "rest"), 0, 0, tiled=True)
    prepared = call(
        prepare_kernel,
        [
            flat_shape,
            flat_shape,
            jax.ShapeDtypeStruct((4 * hidden, chans), BF16),
            jax.ShapeDtypeStruct((2, hidden, LANES), F32),
        ],
        [padded, pltpu.VMEM(flat_shape.shape, F32), pltpu.VMEM(flat_shape.shape, F32), pltpu.SemaphoreType.DMA((3,))],
        gate_flops,
        pair, norm_in_gain, w_gate, w_proj, norm_out_gain,
        pinned=[pltpu.HBM] + [None] * 4, spaces=[pltpu.HBM, pltpu.HBM, None, None],
    )
    recv, (ordered, gate, w_t, gain_cols) = lax.optimization_barrier((recv, prepared))
    half_scratch = [
        pltpu.VMEM((rest * second, total), BF16),
        pltpu.VMEM((rest * second, total), BF16),
        pltpu.VMEM((rest // 2, rows, 2, 4 * shared, n1, LANES), BF16),
    ]
    (product,) = call(
        functools.partial(outgoing_kernel, cols, first, shared),
        [shaped(ndev, depth + 2 * shared)],
        [pltpu.VMEM((cols * second, total), BF16)] * 2 + (half_scratch if shared else []),
        tri_flops, recv, *(spread(*swaps) if shared else []),
    )
    summed = lax.all_to_all(product, ("row", "half", "rest"), 0, 0, tiled=True)
    send_shape, b_shape = shaped(rows, 2, rest, half_depth), shaped(rows, rest // 2, half_depth)
    middle, send, keep, swap = call(
        middle_kernel,
        [flat_shape, send_shape, b_shape, b_shape],
        [
            normal,
            planes,
            pltpu.VMEM(flat_shape.shape, F32),
            pltpu.VMEM(send_shape.shape, BF16),
            pltpu.VMEM((2,) + b_shape.shape, BF16),
            pltpu.SemaphoreType.DMA((5,)),
        ],
        proj_flops + gate_flops,
        ordered, summed.reshape(rows, 2, rest, depth + 2 * shared, n1, LANES), gate, gain_cols, w_out, norm_in_gain, w_t,
        spaces=[pltpu.HBM] * 4,
    )
    recv = lax.all_to_all(
        send.reshape(ndev, half_depth, n1, LANES), ("row", "half", "rest"), 0, 0, tiled=True
    )
    (gate,) = call(
        gate_kernel, [flat_shape],
        [pltpu.VMEM(flat_shape.shape, F32), pltpu.VMEM(flat_shape.shape, F32), pltpu.SemaphoreType.DMA((2,))],
        gate_flops, middle, norm_in_gain, w_gate,
        pinned=[pltpu.HBM, None, None], spaces=[pltpu.HBM],
    )
    recv, gate = lax.optimization_barrier((recv, gate))
    (product,) = call(
        functools.partial(incoming_kernel, cols, first),
        [shaped(rows * rest, half_depth)],
        [
            pltpu.VMEM((cols * second, total), BF16),
            pltpu.VMEM((rest * second, total), BF16),
            pltpu.VMEM((rest // 2, rows, 2, half_depth, n1, LANES), BF16),
        ],
        tri_flops, recv, *spread(keep, swap),
    )
    summed = lax.all_to_all(product, ("row", "rest"), 0, 0, tiled=True)
    (updated,) = call(
        last_kernel,
        [jax.ShapeDtypeStruct(pair.shape, F32)], [normal, padded, pltpu.SemaphoreType.DMA((1,))], gate_flops,
        middle, summed.reshape(hidden, n1, LANES), gate, gain_cols, w_out, spaces=[pltpu.HBM],
    )
    return updated


def solution(mesh):
    rows, cols = mesh.shape["row"], mesh.shape["col"]
    halved = jax.sharding.Mesh(mesh.devices.reshape(rows, 2, cols // 2), ("row", "half", "rest"))
    block = P("row", ("half", "rest"), None)
    return jax.shard_map(
        functools.partial(body, rows, cols),
        mesh=halved,
        in_specs=(block, P(), P(), P(), P(), P()),
        out_specs=block,
        check_vma=False,
    )
```

```python
import functools

import jax
import jax.numpy as jnp
from jax import lax
from jax.experimental import pallas as pl
from jax.experimental.pallas import tpu as pltpu
from jax.sharding import PartitionSpec as P

LANES = 128
BF16 = jnp.bfloat16
F32 = jnp.float32
VMEM_LIMIT = 16 * 1024 * 1024


def sigmoid(x):
    return 0.5 * jnp.tanh(0.5 * x) + 0.5


def norm_rows(x, gain):
    center = x - jnp.mean(x, axis=-1, keepdims=True)
    spread = jnp.mean(center * center, axis=-1, keepdims=True)
    return (center * lax.rsqrt(spread + 1e-05) * gain).astype(BF16)


def block_rows(first, second):
    split = LANES // first
    n1 = second // split
    return [l * n1 + s for s in range(n1) for l in range(split)]


def load_block(padded, first, second):
    rows = block_rows(first, second)
    return jnp.concatenate([padded[pl.ds(row, first, stride=second + 1), :] for row in rows], axis=0)


def block_copies(hbm, padded, sem):
    first, second, _ = hbm.shape
    return [(hbm.at[f], padded.at[pl.ds(f * (second + 1), second), :], sem) for f in range(first)]


def wait_block(hbm, padded, sem):
    first, second, chans = hbm.shape
    whole = padded.at[pl.ds(0, first * second), :]
    pltpu.make_async_copy(whole, whole, sem).wait()


def branch_planes(normed, w_t, n1, planes):
    hidden = w_t.shape[0] // 4
    pad = n1 + 1
    proj = lax.dot_general(w_t, normed, (((1,), (1,)), ((), ())), preferred_element_type=F32)
    for side in range(2):
        at = 2 * side * hidden
        value = sigmoid(proj[at : at + hidden]) * proj[at + hidden : at + 2 * hidden]
        for s in range(n1):
            planes[pl.ds(side * hidden * pad + s, hidden, stride=pad), :] = value[:, s * LANES : (s + 1) * LANES]


def plane(planes, n1, channel):
    at = channel * (n1 + 1)
    return planes[at : at + n1, :].astype(BF16)


def relative_blocks(b_ref, planes, n1, channels):
    rows, highs = b_ref.shape[1:3]
    my_row, my_rest = lax.axis_index("row"), lax.axis_index("rest")
    for r in range(rows):
        for c in range(2 * highs):
            apart = jnp.bitwise_xor(my_rest, c)
            for i, channel in enumerate(channels(r, c)):
                b_ref[apart % 2, jnp.bitwise_xor(my_row, r), apart // 2, i] = plane(planes, n1, channel)


def project_kernel(shared, pair_hbm, gain_hbm, w_hbm, send_hbm, *refs):
    if shared:
        keep_hbm, swap_hbm, padded, gain_ref, w_ref, planes, send_ref, b_ref, in_sems, out_sems = refs
    else:
        padded, gain_ref, w_ref, planes, send_ref, in_sems, out_sems = refs
    first, second, _ = pair_hbm.shape
    ndev, _, depth, n1, _ = send_ref.shape
    hidden = ndev * (depth + shared)
    copies = [pltpu.make_async_copy(*c) for c in block_copies(pair_hbm, padded, in_sems.at[0])]
    small = [
        pltpu.make_async_copy(gain_hbm, gain_ref, in_sems.at[1]),
        pltpu.make_async_copy(w_hbm.at[0], w_ref, in_sems.at[2]),
    ]
    for copy in small + copies:
        copy.start()
    for copy in small:
        copy.wait()
    wait_block(pair_hbm, padded, in_sems.at[0])
    normed = norm_rows(load_block(padded, first, second), gain_ref[0:1, :])
    branch_planes(normed, w_ref[...].T, n1, planes)
    sent = []

    def leave(vmem, hbm):
        sent.append(pltpu.make_async_copy(vmem, hbm, out_sems.at[len(sent)]))
        sent[-1].start()

    if shared:
        rest = 2 * b_ref.shape[2]

        def channels(r, c):
            at = ndev * depth + (r * rest + c) * 2 * shared
            return [side * hidden + at + h for side in range(2) for h in range(2 * shared)]

        relative_blocks(b_ref, planes, n1, channels)
        leave(b_ref.at[1], swap_hbm)
        leave(b_ref.at[0], keep_hbm)
    for part in range(2):
        own = range(part * ndev // 2, (part + 1) * ndev // 2)
        for device in own:
            for side in range(2):
                for h in range(depth):
                    send_ref[device, side, h] = plane(planes, n1, side * hidden + device * depth + h)
        at = pl.ds(own[0], len(own))
        leave(send_ref.at[at], send_hbm.at[at])
    for copy in sent:
        copy.wait()


def move(copies):
    for copy in copies:
        copy.start()
    for copy in copies:
        copy.wait()


def prepare_kernel(
    pair_hbm, gain_ref, w_gate_ref, w_ref, out_gain_ref,
    ordered_hbm, gate_hbm, w_t_ref, gain_cols_ref, padded, ordered_ref, gate_ref, sems,
):
    first, second, _ = pair_hbm.shape
    for copy in block_copies(pair_hbm, padded, sems.at[0]):
        pltpu.make_async_copy(*copy).start()
    w_t_ref[...] = w_ref[1].T
    for u in range(2):
        wide = (LANES, out_gain_ref.shape[1])
        gain_cols_ref[u] = jnp.broadcast_to(out_gain_ref[u : u + 1, :], wide).T
    wait_block(pair_hbm, padded, sems.at[0])
    x = load_block(padded, first, second)
    ordered_ref[...] = x
    normed = norm_rows(x, gain_ref[0:1, :])
    gate_ref[...] = sigmoid(jnp.dot(normed, w_gate_ref[0], preferred_element_type=F32))
    move([
        pltpu.make_async_copy(ordered_ref, ordered_hbm, sems.at[1]),
        pltpu.make_async_copy(gate_ref, gate_hbm, sems.at[2]),
    ])


def gate_kernel(first_hbm, gain_ref, w_gate_ref, gate_hbm, first_ref, gate_ref, sems):
    move([pltpu.make_async_copy(first_hbm, first_ref, sems.at[0])])
    normed = norm_rows(first_ref[...], gain_ref[1:2, :])
    gate_ref[...] = sigmoid(jnp.dot(normed, w_gate_ref[1], preferred_element_type=F32))
    move([pltpu.make_async_copy(gate_ref, gate_hbm, sems.at[1])])


def stage(part_refs, b_ref):
    rows = b_ref.shape[1]
    for r in range(rows):
        b_ref[0, r] = part_refs[r][...]
    for apart, part_ref in enumerate(part_refs[rows:], 1):
        b_ref[apart] = part_ref[...]


def dense_half(b_ref, i, first, dense):
    highs, rows, _, _, n1, _ = b_ref.shape
    split = LANES // first
    my_row, my_rest = lax.axis_index("row"), lax.axis_index("rest")
    for c in range(2 * highs):
        apart = jnp.bitwise_xor(my_rest, c)
        for l in range(split):
            at = (c * split + l) * n1
            dense[at : at + n1, :] = jnp.concatenate(
                [
                    b_ref[apart // 2, jnp.bitwise_xor(my_row, r), apart % 2, i, :, l * first : (l + 1) * first]
                    for r in range(rows)
                ],
                axis=1,
            )


def transposed_product(left, right):
    return lax.dot_general(
        right[...], left[...], (((0,), (0,)), ((), ())), preferred_element_type=F32
    ).astype(BF16)


def outgoing_half_kernel(cols, first, *refs):
    *part_refs, out_ref, left, right, b_ref = refs
    rows, depth = out_ref.shape[0] // cols, out_ref.shape[1]
    stage(part_refs, b_ref)
    for h in range(depth):
        dense_half(b_ref, h, first, left)
        dense_half(b_ref, depth + h, first, right)
        scatter_product(transposed_product(left, right), rows, cols, first, h, out_ref)


def outgoing_kernel(cols, first, recv_ref, *refs):
    *half_ref, out_ref, left, right = refs
    ndev, _, depth, n1, _ = recv_ref.shape
    split = LANES // first
    rows = ndev // cols
    for h in range(depth):
        for side, dense in ((0, left), (1, right)):
            for c in range(cols):
                for l in range(split):
                    at = (c * split + l) * n1
                    dense[at : at + n1, :] = jnp.concatenate(
                        [
                            recv_ref[r * cols + c, side, h, :, l * first : (l + 1) * first]
                            for r in range(rows)
                        ],
                        axis=1,
                    )
        scatter_product(transposed_product(left, right), rows, cols, first, h, out_ref)
    for ref in half_ref:
        out_ref[:, depth:] = ref[...]


def scatter_product(summed, rows, cols, first, h, out_ref):
    split = LANES // first
    n1 = out_ref.shape[2]
    for r in range(rows):
        for c in range(cols):
            out_ref[r * cols + c, h] = jnp.concatenate(
                [
                    summed[(c * split + l) * n1 : (c * split + l + 1) * n1, r * first : (r + 1) * first]
                    for l in range(split)
                ],
                axis=1,
            )


def incoming_layout_kernel(first, *refs):
    *part_refs, dense_ref, b_ref = refs
    stage(part_refs, b_ref)
    for h in range(dense_ref.shape[0]):
        dense_half(b_ref, h, first, dense_ref.at[h])


def incoming_kernel(cols, first, recv_ref, dense_ref, out_ref, left):
    ndev, depth, n1, _ = recv_ref.shape
    split = LANES // first
    rows = ndev // cols
    for h in range(depth):
        for c in range(cols):
            for l in range(split):
                at = (c * split + l) * n1
                left[at : at + n1, :] = jnp.concatenate(
                    [recv_ref[r * cols + c, h, :, l * first : (l + 1) * first] for r in range(rows)], axis=1
                )
        summed = lax.dot_general(
            dense_ref[h], left[...], (((1,), (1,)), ((), ())), preferred_element_type=F32
        ).astype(BF16)
        scatter_product(summed, rows, cols // 2, first, h, out_ref)


def output(x, gain_cols, w, normal):
    hidden, n1, _ = x.shape
    pad = n1 + 1
    center = x - jnp.mean(x, axis=0, keepdims=True)
    spread = jnp.mean(center * center, axis=0, keepdims=True)
    scaled = center * lax.rsqrt(spread + 1e-05)
    for h in range(hidden):
        normal[h * pad : h * pad + n1, :] = scaled[h]
    mixed = jnp.concatenate(
        [(normal[pl.ds(s, hidden, stride=pad), :] * gain_cols).astype(BF16) for s in range(n1)], axis=1
    )
    return lax.dot_general(mixed, w, (((0,), (0,)), ((), ())), preferred_element_type=F32)


def middle_kernel(
    ordered_ref, summed_ref, gate_ref, gain_cols_ref, w_out_ref, gain_ref, w_t_ref,
    first_hbm, send_hbm, keep_hbm, swap_hbm, normal, planes, first_ref, send_ref, b_ref, sems,
):
    rows, rest, depth, n1, _ = send_ref.shape
    halves = send_hbm.shape[1]
    hidden = rows * rest * depth
    copies = []

    def leave(vmem, hbm):
        copies.append(pltpu.make_async_copy(vmem, hbm, sems.at[len(copies)]))
        copies[-1].start()

    shared = summed_ref.shape[3] - depth // 2
    own = summed_ref.shape[3] - 2 * shared
    x = summed_ref[:, :, :, :own].astype(F32).reshape(-1, n1, LANES)
    if shared:
        x_shared = summed_ref[:, 0, :, own:].astype(F32) + summed_ref[:, 1, :, own:].astype(F32)
        x = jnp.concatenate([x, x_shared.reshape(-1, n1, LANES)], axis=0)
    z = ordered_ref[...] + gate_ref[...] * output(x, gain_cols_ref[0], w_out_ref[0], normal)
    first_ref[...] = z
    leave(first_ref, first_hbm)
    branch_planes(norm_rows(z, gain_ref[1:2, :]), w_t_ref[...], n1, planes)
    relative_blocks(
        b_ref, planes, n1, lambda r, c: [hidden + (r * rest + c) * depth + h for h in range(depth)]
    )
    leave(b_ref.at[1], swap_hbm)
    leave(b_ref.at[0], keep_hbm)
    for r in range(rows):
        for c in range(rest):
            for h in range(depth):
                send_ref[r, c, h] = plane(planes, n1, (r * rest + c) * depth + h)
        if r % (rows // 2) == rows // 2 - 1:
            own = pl.ds(r + 1 - rows // 2, rows // 2)
            for half in range(halves):
                leave(send_ref.at[own], send_hbm.at[own, half])
    for copy in copies:
        copy.wait()


def last_kernel(
    first_ref, summed_ref, gate_ref, gain_cols_ref, w_out_ref, updated_hbm, normal, padded, sems
):
    first, second, _ = updated_hbm.shape
    z = first_ref[...] + gate_ref[...] * output(summed_ref[...].astype(F32), gain_cols_ref[1], w_out_ref[1], normal)
    for i, row in enumerate(block_rows(first, second)):
        padded[pl.ds(row, first, stride=second + 1), :] = z[i * first : (i + 1) * first]
    copies = [
        pltpu.make_async_copy(vmem, hbm, sem) for hbm, vmem, sem in block_copies(updated_hbm, padded, sems.at[0])
    ]
    for copy in copies:
        copy.start()
    wait_block(updated_hbm, padded, sems.at[0])


def call(kernel, outs, scratch, flops, *args, pinned=None, spaces=None):
    moved = sum(a.size * a.dtype.itemsize for a in args) + sum(o.size * o.dtype.itemsize for o in outs)
    pinned = pinned or [None] * len(args)
    spaces = spaces or [None] * len(outs)
    args = [a if space is None else pltpu.with_memory_space_constraint(a, space) for a, space in zip(args, pinned)]
    outs = [o if space is None else space(o.shape, o.dtype) for o, space in zip(outs, spaces)]
    in_specs = [pl.BlockSpec(memory_space=space or pltpu.VMEM) for space in pinned]
    out_specs = [pl.BlockSpec(memory_space=space or pltpu.VMEM) for space in spaces]
    return pl.pallas_call(
        kernel,
        out_shape=outs,
        in_specs=in_specs,
        out_specs=out_specs,
        scratch_shapes=scratch,
        compiler_params=pltpu.CompilerParams(vmem_limit_bytes=VMEM_LIMIT),
        cost_estimate=pl.CostEstimate(flops=flops, bytes_accessed=moved, transcendentals=0),
    )(*args)


def spread(keep, swap):
    rows, highs = keep.shape[:2]
    rest = 2 * highs

    def swapped(x, axis, size, apart):
        return lax.ppermute(x, axis, [(d, d ^ apart) for d in range(size)]) if apart else x

    b = jnp.stack([keep, swapped(swap, "rest", rest, 1)], axis=2)
    far = [
        swapped(jnp.stack([swapped(b[r, c], "row", rows, r) for r in range(rows)]), "rest", rest, 2 * c)
        for c in range(1, highs)
    ]
    return [swapped(b[r, 0], "row", rows, r) for r in range(rows)] + far


def body(rows, cols, pair, norm_in_gain, w_proj, w_gate, norm_out_gain, w_out):
    first, second, chans = pair.shape
    hidden = w_out.shape[1]
    ndev = rows * cols
    rest = cols // 2
    shared = hidden // ndev // 4
    depth, half_depth = hidden // ndev - shared, 2 * hidden // ndev
    count = first * second
    n1 = count // LANES
    total = rows * first

    flat_shape = jax.ShapeDtypeStruct((count, chans), F32)
    planes = pltpu.VMEM((2 * hidden * (n1 + 1), LANES), F32)
    normal = pltpu.VMEM((hidden * (n1 + 1), LANES), F32)
    padded = pltpu.VMEM((first * (second + 1), chans), F32)
    proj_flops = 2 * count * chans * 4 * hidden
    gate_flops = 2 * count * chans * chans
    tri_flops = 2 * (depth + shared) * total**3

    def shaped(*shape):
        return jax.ShapeDtypeStruct(shape + (n1, LANES), BF16)

    out_shapes = [shaped(ndev, 2, depth)] + [shaped(rows, rest // 2, 4 * shared)] * (2 if shared else 0)
    send, *swaps = call(
        functools.partial(project_kernel, shared),
        out_shapes,
        [
            padded,
            pltpu.VMEM(norm_in_gain.shape, F32),
            pltpu.VMEM(w_proj.shape[1:], BF16),
            planes,
            pltpu.VMEM(out_shapes[0].shape, BF16),
        ]
        + ([pltpu.VMEM((2,) + out_shapes[1].shape, BF16)] if shared else [])
        + [pltpu.SemaphoreType.DMA((3,)), pltpu.SemaphoreType.DMA((4,))],
        proj_flops, pair, norm_in_gain, w_proj,
        pinned=[pltpu.HBM] * 3, spaces=[pltpu.HBM] * len(out_shapes),
    )
    recv = lax.all_to_all(send, ("row", "half", "rest"), 0, 0, tiled=True)
    prepared = call(
        prepare_kernel,
        [
            flat_shape,
            flat_shape,
            jax.ShapeDtypeStruct((4 * hidden, chans), BF16),
            jax.ShapeDtypeStruct((2, hidden, LANES), F32),
        ],
        [padded, pltpu.VMEM(flat_shape.shape, F32), pltpu.VMEM(flat_shape.shape, F32), pltpu.SemaphoreType.DMA((3,))],
        gate_flops,
        pair, norm_in_gain, w_gate, w_proj, norm_out_gain,
        pinned=[pltpu.HBM] + [None] * 4, spaces=[pltpu.HBM, pltpu.HBM, None, None],
    )
    halves = []
    if shared:
        halves = call(
            functools.partial(outgoing_half_kernel, cols, first),
            [shaped(ndev, 2 * shared)],
            [
                pltpu.VMEM((rest * second, total), BF16),
                pltpu.VMEM((rest * second, total), BF16),
                pltpu.VMEM((rest // 2, rows, 2, 4 * shared, n1, LANES), BF16),
            ],
            tri_flops // 4, *spread(*swaps),
        )
    recv, halves, (ordered, gate, w_t, gain_cols) = lax.optimization_barrier((recv, halves, prepared))
    (product,) = call(
        functools.partial(outgoing_kernel, cols, first),
        [shaped(ndev, depth + 2 * shared)],
        [pltpu.VMEM((cols * second, total), BF16)] * 2,
        tri_flops, recv, *halves,
    )
    summed = lax.all_to_all(product, ("row", "half", "rest"), 0, 0, tiled=True)
    send_shape, b_shape = shaped(rows, 2, rest, half_depth), shaped(rows, rest // 2, half_depth)
    middle, send, keep, swap = call(
        middle_kernel,
        [flat_shape, send_shape, b_shape, b_shape],
        [
            normal,
            planes,
            pltpu.VMEM(flat_shape.shape, F32),
            pltpu.VMEM((rows, rest, half_depth, n1, LANES), BF16),
            pltpu.VMEM((2,) + b_shape.shape, BF16),
            pltpu.SemaphoreType.DMA((7,)),
        ],
        proj_flops + gate_flops,
        ordered, summed.reshape(rows, 2, rest, depth + 2 * shared, n1, LANES), gate, gain_cols, w_out, norm_in_gain, w_t,
        spaces=[pltpu.HBM] * 4,
    )
    recv = lax.all_to_all(
        send.reshape(ndev, half_depth, n1, LANES), ("row", "half", "rest"), 0, 0, tiled=True
    )
    (gate,) = call(
        gate_kernel, [flat_shape],
        [pltpu.VMEM(flat_shape.shape, F32), pltpu.VMEM(flat_shape.shape, F32), pltpu.SemaphoreType.DMA((2,))],
        gate_flops, middle, norm_in_gain, w_gate,
        pinned=[pltpu.HBM, None, None], spaces=[pltpu.HBM],
    )
    dense = call(
        functools.partial(incoming_layout_kernel, first),
        [jax.ShapeDtypeStruct((half_depth, rest * second, total), BF16)],
        [pltpu.VMEM((rest // 2, rows, 2, half_depth, n1, LANES), BF16)],
        0, *spread(keep, swap),
    )
    recv, gate, dense = lax.optimization_barrier((recv, gate, dense))
    (product,) = call(
        functools.partial(incoming_kernel, cols, first),
        [shaped(rows * rest, half_depth)], [pltpu.VMEM((cols * second, total), BF16)],
        tri_flops, recv, *dense,
    )
    summed = lax.all_to_all(product, ("row", "rest"), 0, 0, tiled=True)
    (updated,) = call(
        last_kernel,
        [jax.ShapeDtypeStruct(pair.shape, F32)], [normal, padded, pltpu.SemaphoreType.DMA((1,))], gate_flops,
        middle, summed.reshape(hidden, n1, LANES), gate, gain_cols, w_out, spaces=[pltpu.HBM],
    )
    return updated


def solution(mesh):
    rows, cols = mesh.shape["row"], mesh.shape["col"]
    halved = jax.sharding.Mesh(mesh.devices.reshape(rows, 2, cols // 2), ("row", "half", "rest"))
    block = P("row", ("half", "rest"), None)
    return jax.shard_map(
        functools.partial(body, rows, cols),
        mesh=halved,
        in_specs=(block, P(), P(), P(), P(), P()),
        out_specs=block,
        check_vma=False,
    )
```

```python
import functools

import jax
import jax.numpy as jnp
from jax import lax
from jax.experimental import pallas as pl
from jax.experimental.pallas import tpu as pltpu
from jax.sharding import PartitionSpec as P

LANES = 128
BF16 = jnp.bfloat16
F32 = jnp.float32
VMEM_LIMIT = 16 * 1024 * 1024


def sigmoid(x):
    return 0.5 * jnp.tanh(0.5 * x) + 0.5


def norm_rows(x, gain):
    center = x - jnp.mean(x, axis=-1, keepdims=True)
    spread = jnp.mean(center * center, axis=-1, keepdims=True)
    return (center * lax.rsqrt(spread + 1e-05) * gain).astype(BF16)


def block_rows(first, second):
    split = LANES // first
    n1 = second // split
    return [l * n1 + s for s in range(n1) for l in range(split)]


def load_block(padded, first, second):
    rows = block_rows(first, second)
    return jnp.concatenate([padded[pl.ds(row, first, stride=second + 1), :] for row in rows], axis=0)


def block_copies(hbm, padded, sem):
    first, second, _ = hbm.shape
    return [(hbm.at[f], padded.at[pl.ds(f * (second + 1), second), :], sem) for f in range(first)]


def wait_block(hbm, padded, sem):
    first, second, chans = hbm.shape
    whole = padded.at[pl.ds(0, first * second), :]
    pltpu.make_async_copy(whole, whole, sem).wait()


def branch_planes(normed, w_t, n1, planes):
    hidden = w_t.shape[0] // 4
    pad = n1 + 1
    proj = lax.dot_general(w_t, normed, (((1,), (1,)), ((), ())), preferred_element_type=F32)
    for side in range(2):
        at = 2 * side * hidden
        value = sigmoid(proj[at : at + hidden]) * proj[at + hidden : at + 2 * hidden]
        for s in range(n1):
            planes[pl.ds(side * hidden * pad + s, hidden, stride=pad), :] = value[:, s * LANES : (s + 1) * LANES]


def plane(planes, n1, channel):
    at = channel * (n1 + 1)
    return planes[at : at + n1, :].astype(BF16)


def leave_blocks(b_ref, keep_hbm, swap_hbm, sem):
    my_row, my_rest = lax.axis_index("row"), lax.axis_index("rest")
    for core, hbm in ((1, swap_hbm), (0, keep_hbm)):
        for r in range(hbm.shape[0]):
            for c in range(hbm.shape[1]):
                block = b_ref.at[jnp.bitwise_xor(my_row, r), jnp.bitwise_xor(my_rest, 2 * c + core)]
                pltpu.make_async_copy(block, hbm.at[r, c], sem).start()
    return pltpu.make_async_copy(b_ref, b_ref, sem)


def project_kernel(shared, pair_hbm, gain_hbm, w_hbm, send_hbm, *refs):
    if shared:
        keep_hbm, swap_hbm, padded, gain_ref, w_ref, planes, send_ref, b_ref, in_sems, out_sems = refs
    else:
        padded, gain_ref, w_ref, planes, send_ref, in_sems, out_sems = refs
    first, second, _ = pair_hbm.shape
    ndev, _, depth, n1, _ = send_ref.shape
    hidden = ndev * (depth + shared)
    copies = [pltpu.make_async_copy(*c) for c in block_copies(pair_hbm, padded, in_sems.at[0])]
    small = [
        pltpu.make_async_copy(gain_hbm, gain_ref, in_sems.at[1]),
        pltpu.make_async_copy(w_hbm.at[0], w_ref, in_sems.at[2]),
    ]
    for copy in small + copies:
        copy.start()
    for copy in small:
        copy.wait()
    wait_block(pair_hbm, padded, in_sems.at[0])
    normed = norm_rows(load_block(padded, first, second), gain_ref[0:1, :])
    branch_planes(normed, w_ref[...].T, n1, planes)
    sent = []

    def leave(vmem, hbm, sem):
        sent.append(pltpu.make_async_copy(vmem, hbm, sem))
        sent[-1].start()

    if shared:
        rows, rest = b_ref.shape[:2]
        for r in range(rows):
            for c in range(rest):
                at = ndev * depth + (r * rest + c) * 2 * shared
                for side in range(2):
                    for h in range(2 * shared):
                        b_ref[r, c, 2 * shared * side + h] = plane(planes, n1, side * hidden + at + h)
        sent.append(leave_blocks(b_ref, keep_hbm, swap_hbm, out_sems.at[2]))
    for part in range(2):
        own = range(part * ndev // 2, (part + 1) * ndev // 2)
        for device in own:
            for side in range(2):
                for h in range(depth):
                    send_ref[device, side, h] = plane(planes, n1, side * hidden + device * depth + h)
        at = pl.ds(own[0], len(own))
        leave(send_ref.at[at], send_hbm.at[at], out_sems.at[part])
    for copy in sent:
        copy.wait()


def move(copies):
    for copy in copies:
        copy.start()
    for copy in copies:
        copy.wait()


def prepare_kernel(
    pair_hbm, gain_ref, w_gate_ref, w_ref, out_gain_ref,
    ordered_hbm, gate_hbm, w_t_ref, gain_cols_ref, padded, ordered_ref, gate_ref, sems,
):
    first, second, _ = pair_hbm.shape
    for copy in block_copies(pair_hbm, padded, sems.at[0]):
        pltpu.make_async_copy(*copy).start()
    w_t_ref[...] = w_ref[1].T
    for u in range(2):
        wide = (LANES, out_gain_ref.shape[1])
        gain_cols_ref[u] = jnp.broadcast_to(out_gain_ref[u : u + 1, :], wide).T
    wait_block(pair_hbm, padded, sems.at[0])
    x = load_block(padded, first, second)
    ordered_ref[...] = x
    normed = norm_rows(x, gain_ref[0:1, :])
    gate_ref[...] = sigmoid(jnp.dot(normed, w_gate_ref[0], preferred_element_type=F32))
    move([
        pltpu.make_async_copy(ordered_ref, ordered_hbm, sems.at[1]),
        pltpu.make_async_copy(gate_ref, gate_hbm, sems.at[2]),
    ])


def gate_kernel(first_hbm, gain_ref, w_gate_ref, gate_hbm, first_ref, gate_ref, sems):
    move([pltpu.make_async_copy(first_hbm, first_ref, sems.at[0])])
    normed = norm_rows(first_ref[...], gain_ref[1:2, :])
    gate_ref[...] = sigmoid(jnp.dot(normed, w_gate_ref[1], preferred_element_type=F32))
    move([pltpu.make_async_copy(gate_ref, gate_hbm, sems.at[1])])


def stage(part_refs, b_ref):
    rows = b_ref.shape[1]
    for r in range(rows):
        b_ref[0, r] = part_refs[r][...]
    for apart, part_ref in enumerate(part_refs[rows:], 1):
        b_ref[apart] = part_ref[...]


def dense_half(b_ref, i, first, dense):
    highs, rows, _, _, n1, _ = b_ref.shape
    split = LANES // first
    my_row, my_rest = lax.axis_index("row"), lax.axis_index("rest")
    for c in range(2 * highs):
        apart = jnp.bitwise_xor(my_rest, c)
        for l in range(split):
            at = (c * split + l) * n1
            dense[at : at + n1, :] = jnp.concatenate(
                [
                    b_ref[apart // 2, jnp.bitwise_xor(my_row, r), apart % 2, i, :, l * first : (l + 1) * first]
                    for r in range(rows)
                ],
                axis=1,
            )


def transposed_product(left, right):
    return lax.dot_general(
        right[...], left[...], (((0,), (0,)), ((), ())), preferred_element_type=F32
    ).astype(BF16)


def outgoing_half_kernel(cols, first, *refs):
    *part_refs, out_ref, left, right, b_ref = refs
    rows, depth = out_ref.shape[0] // cols, out_ref.shape[1]
    places = [[slot(cols, r, c) for c in range(cols)] for r in range(rows)]
    stage(part_refs, b_ref)
    for h in range(depth):
        dense_half(b_ref, h, first, left)
        dense_half(b_ref, depth + h, first, right)
        scatter_product(transposed_product(left, right), first, h, places, out_ref)


def outgoing_kernel(cols, first, recv_ref, *refs):
    *half_ref, out_ref, left, right = refs
    ndev, _, depth, n1, _ = recv_ref.shape
    split = LANES // first
    rows = ndev // cols
    places = [[slot(cols, r, c) for c in range(cols)] for r in range(rows)]
    for h in range(depth):
        for side, dense in ((0, left), (1, right)):
            for c in range(cols):
                for l in range(split):
                    at = (c * split + l) * n1
                    dense[at : at + n1, :] = jnp.concatenate(
                        [
                            recv_ref[places[r][c], side, h, :, l * first : (l + 1) * first]
                            for r in range(rows)
                        ],
                        axis=1,
                    )
        scatter_product(transposed_product(left, right), first, h, places, out_ref)
    for ref in half_ref:
        out_ref[:, depth:] = ref[...]


def slot(cols, r, c):
    rest = cols // 2
    return (r * rest + c % rest) * 2 + c // rest


def scatter_product(summed, first, h, places, out_ref):
    split = LANES // first
    n1 = out_ref.shape[2]
    for r, row in enumerate(places):
        for c, place in enumerate(row):
            out_ref[place, h] = jnp.concatenate(
                [
                    summed[(c * split + l) * n1 : (c * split + l + 1) * n1, r * first : (r + 1) * first]
                    for l in range(split)
                ],
                axis=1,
            )


def incoming_layout_kernel(first, *refs):
    *part_refs, dense_ref, b_ref = refs
    stage(part_refs, b_ref)
    for h in range(dense_ref.shape[0]):
        dense_half(b_ref, h, first, dense_ref.at[h])


def incoming_kernel(cols, first, recv_ref, dense_ref, out_ref, left):
    ndev, depth, n1, _ = recv_ref.shape
    split = LANES // first
    rows = ndev // cols
    places = [[c * rows + r for c in range(cols // 2)] for r in range(rows)]
    for h in range(depth):
        for c in range(cols):
            for l in range(split):
                at = (c * split + l) * n1
                left[at : at + n1, :] = jnp.concatenate(
                    [recv_ref[slot(cols, r, c), h, :, l * first : (l + 1) * first] for r in range(rows)], axis=1
                )
        summed = lax.dot_general(
            dense_ref[h], left[...], (((1,), (1,)), ((), ())), preferred_element_type=F32
        ).astype(BF16)
        scatter_product(summed, first, h, places, out_ref)


def output(x, gain_cols, w, normal):
    hidden, n1, _ = x.shape
    pad = n1 + 1
    center = x - jnp.mean(x, axis=0, keepdims=True)
    spread = jnp.mean(center * center, axis=0, keepdims=True)
    scaled = center * lax.rsqrt(spread + 1e-05)
    for h in range(hidden):
        normal[h * pad : h * pad + n1, :] = scaled[h]
    mixed = jnp.concatenate(
        [(normal[pl.ds(s, hidden, stride=pad), :] * gain_cols).astype(BF16) for s in range(n1)], axis=1
    )
    return lax.dot_general(mixed, w, (((0,), (0,)), ((), ())), preferred_element_type=F32)


def middle_kernel(
    ordered_ref, summed_ref, gate_ref, gain_cols_ref, w_out_ref, gain_ref, w_t_ref,
    first_hbm, send_hbm, keep_hbm, swap_hbm, normal, planes, first_ref, send_ref, b_ref, sems,
):
    rows, rest, depth, n1, _ = send_ref.shape
    halves = send_hbm.shape[2]
    hidden = rows * rest * depth
    copies = []

    def leave(vmem, hbm):
        copies.append(pltpu.make_async_copy(vmem, hbm, sems.at[len(copies)]))
        copies[-1].start()

    shared = summed_ref.shape[3] - depth // 2
    own = summed_ref.shape[3] - 2 * shared
    x = summed_ref[:, :, :, :own].astype(F32).reshape(-1, n1, LANES)
    if shared:
        x_shared = summed_ref[:, :, 0, own:].astype(F32) + summed_ref[:, :, 1, own:].astype(F32)
        x = jnp.concatenate([x, x_shared.reshape(-1, n1, LANES)], axis=0)
    z = ordered_ref[...] + gate_ref[...] * output(x, gain_cols_ref[0], w_out_ref[0], normal)
    first_ref[...] = z
    leave(first_ref, first_hbm)
    branch_planes(norm_rows(z, gain_ref[1:2, :]), w_t_ref[...], n1, planes)
    for r in range(rows):
        for c in range(rest):
            for h in range(depth):
                b_ref[r, c, h] = plane(planes, n1, hidden + (c * rows + r) * depth + h)
    copies.append(leave_blocks(b_ref, keep_hbm, swap_hbm, sems.at[len(copies)]))
    for r in range(rows):
        for c in range(rest):
            for h in range(depth):
                send_ref[r, c, h] = plane(planes, n1, (c * rows + r) * depth + h)
        if r % (rows // 2) == rows // 2 - 1:
            own = pl.ds(r + 1 - rows // 2, rows // 2)
            for half in range(halves):
                leave(send_ref.at[own], send_hbm.at[own, :, half])
    for copy in copies:
        copy.wait()


def last_kernel(
    first_ref, summed_ref, gate_ref, gain_cols_ref, w_out_ref, updated_hbm, normal, padded, sems
):
    first, second, _ = updated_hbm.shape
    z = first_ref[...] + gate_ref[...] * output(summed_ref[...].astype(F32), gain_cols_ref[1], w_out_ref[1], normal)
    for i, row in enumerate(block_rows(first, second)):
        padded[pl.ds(row, first, stride=second + 1), :] = z[i * first : (i + 1) * first]
    copies = [
        pltpu.make_async_copy(vmem, hbm, sem) for hbm, vmem, sem in block_copies(updated_hbm, padded, sems.at[0])
    ]
    for copy in copies:
        copy.start()
    wait_block(updated_hbm, padded, sems.at[0])


def call(kernel, outs, scratch, flops, *args, pinned=None, spaces=None):
    moved = sum(a.size * a.dtype.itemsize for a in args) + sum(o.size * o.dtype.itemsize for o in outs)
    pinned = pinned or [None] * len(args)
    spaces = spaces or [None] * len(outs)
    args = [a if space is None else pltpu.with_memory_space_constraint(a, space) for a, space in zip(args, pinned)]
    outs = [o if space is None else space(o.shape, o.dtype) for o, space in zip(outs, spaces)]
    in_specs = [pl.BlockSpec(memory_space=space or pltpu.VMEM) for space in pinned]
    out_specs = [pl.BlockSpec(memory_space=space or pltpu.VMEM) for space in spaces]
    return pl.pallas_call(
        kernel,
        out_shape=outs,
        in_specs=in_specs,
        out_specs=out_specs,
        scratch_shapes=scratch,
        compiler_params=pltpu.CompilerParams(vmem_limit_bytes=VMEM_LIMIT),
        cost_estimate=pl.CostEstimate(flops=flops, bytes_accessed=moved, transcendentals=0),
    )(*args)


def spread(keep, swap):
    rows, highs = keep.shape[:2]
    rest = 2 * highs

    def swapped(x, axis, size, apart):
        return lax.ppermute(x, axis, [(d, d ^ apart) for d in range(size)]) if apart else x

    b = jnp.stack([keep, swapped(swap, "rest", rest, 1)], axis=2)
    far = [
        swapped(jnp.stack([swapped(b[r, c], "row", rows, r) for r in range(rows)]), "rest", rest, 2 * c)
        for c in range(1, highs)
    ]
    return [swapped(b[r, 0], "row", rows, r) for r in range(rows)] + far


def body(rows, cols, pair, norm_in_gain, w_proj, w_gate, norm_out_gain, w_out):
    first, second, chans = pair.shape
    hidden = w_out.shape[1]
    ndev = rows * cols
    rest = cols // 2
    shared = hidden // ndev // 4
    depth, half_depth = hidden // ndev - shared, 2 * hidden // ndev
    count = first * second
    n1 = count // LANES
    total = rows * first

    flat_shape = jax.ShapeDtypeStruct((count, chans), F32)
    planes = pltpu.VMEM(((2 * hidden + 1) * (n1 + 1), LANES), F32)
    normal = pltpu.VMEM(((hidden + 1) * (n1 + 1), LANES), F32)
    padded = pltpu.VMEM(((first + 1) * (second + 1), chans), F32)
    proj_flops = 2 * count * chans * 4 * hidden
    gate_flops = 2 * count * chans * chans
    tri_flops = 2 * (depth + shared) * total**3

    def shaped(*shape):
        return jax.ShapeDtypeStruct(shape + (n1, LANES), BF16)

    out_shapes = [shaped(ndev, 2, depth)] + [shaped(rows, rest // 2, 4 * shared)] * (2 if shared else 0)
    send, *swaps = call(
        functools.partial(project_kernel, shared),
        out_shapes,
        [
            padded,
            pltpu.VMEM(norm_in_gain.shape, F32),
            pltpu.VMEM(w_proj.shape[1:], BF16),
            planes,
            pltpu.VMEM(out_shapes[0].shape, BF16),
        ]
        + ([pltpu.VMEM((rows, rest, 4 * shared, n1, LANES), BF16)] if shared else [])
        + [pltpu.SemaphoreType.DMA((3,)), pltpu.SemaphoreType.DMA((3,))],
        proj_flops, pair, norm_in_gain, w_proj,
        pinned=[pltpu.HBM] * 3, spaces=[pltpu.HBM] * len(out_shapes),
    )
    recv = lax.all_to_all(send, ("row", "rest", "half"), 0, 0, tiled=True)
    prepared = call(
        prepare_kernel,
        [
            flat_shape,
            flat_shape,
            jax.ShapeDtypeStruct((4 * hidden, chans), BF16),
            jax.ShapeDtypeStruct((2, hidden, LANES), F32),
        ],
        [padded, pltpu.VMEM(flat_shape.shape, F32), pltpu.VMEM(flat_shape.shape, F32), pltpu.SemaphoreType.DMA((3,))],
        gate_flops,
        pair, norm_in_gain, w_gate, w_proj, norm_out_gain,
        pinned=[pltpu.HBM] + [None] * 4, spaces=[pltpu.HBM, pltpu.HBM, None, None],
    )
    halves = []
    if shared:
        halves = call(
            functools.partial(outgoing_half_kernel, cols, first),
            [shaped(ndev, 2 * shared)],
            [
                pltpu.VMEM((rest * second, total), BF16),
                pltpu.VMEM((rest * second, total), BF16),
                pltpu.VMEM((rest // 2, rows, 2, 4 * shared, n1, LANES), BF16),
            ],
            tri_flops // 4, *spread(*swaps),
        )
    recv, halves, (ordered, gate, w_t, gain_cols) = lax.optimization_barrier((recv, halves, prepared))
    (product,) = call(
        functools.partial(outgoing_kernel, cols, first),
        [shaped(ndev, depth + 2 * shared)],
        [pltpu.VMEM((cols * second, total), BF16)] * 2,
        tri_flops, recv, *halves,
    )
    summed = lax.all_to_all(product, ("row", "rest", "half"), 0, 0, tiled=True)
    send_shape, b_shape = shaped(rows, rest, 2, half_depth), shaped(rows, rest // 2, half_depth)
    middle, send, keep, swap = call(
        middle_kernel,
        [flat_shape, send_shape, b_shape, b_shape],
        [
            normal,
            planes,
            pltpu.VMEM(flat_shape.shape, F32),
            pltpu.VMEM((rows, rest, half_depth, n1, LANES), BF16),
            pltpu.VMEM((rows, rest, half_depth, n1, LANES), BF16),
            pltpu.SemaphoreType.DMA((6,)),
        ],
        proj_flops + gate_flops,
        ordered, summed.reshape(rows, rest, 2, depth + 2 * shared, n1, LANES), gate, gain_cols, w_out, norm_in_gain, w_t,
        spaces=[pltpu.HBM] * 4,
    )
    recv = lax.all_to_all(
        send.reshape(ndev, half_depth, n1, LANES), ("row", "rest", "half"), 0, 0, tiled=True
    )
    (gate,) = call(
        gate_kernel, [flat_shape],
        [pltpu.VMEM(flat_shape.shape, F32), pltpu.VMEM(flat_shape.shape, F32), pltpu.SemaphoreType.DMA((2,))],
        gate_flops, middle, norm_in_gain, w_gate,
        pinned=[pltpu.HBM, None, None], spaces=[pltpu.HBM],
    )
    dense = call(
        functools.partial(incoming_layout_kernel, first),
        [jax.ShapeDtypeStruct((half_depth, rest * second, total), BF16)],
        [pltpu.VMEM((rest // 2, rows, 2, half_depth, n1, LANES), BF16)],
        0, *spread(keep, swap),
    )
    recv, gate, dense = lax.optimization_barrier((recv, gate, dense))
    (product,) = call(
        functools.partial(incoming_kernel, cols, first),
        [shaped(rows * rest, half_depth)], [pltpu.VMEM((cols * second, total), BF16)],
        tri_flops, recv, *dense,
    )
    summed = lax.all_to_all(product, ("rest", "row"), 0, 0, tiled=True)
    (updated,) = call(
        last_kernel,
        [jax.ShapeDtypeStruct(pair.shape, F32)], [normal, padded, pltpu.SemaphoreType.DMA((1,))], gate_flops,
        middle, summed.reshape(hidden, n1, LANES), gate, gain_cols, w_out, spaces=[pltpu.HBM],
    )
    return updated


def solution(mesh):
    rows, cols = mesh.shape["row"], mesh.shape["col"]
    halved = jax.sharding.Mesh(mesh.devices.reshape(rows, 2, cols // 2), ("row", "half", "rest"))
    block = P("row", ("half", "rest"), None)
    return jax.shard_map(
        functools.partial(body, rows, cols),
        mesh=halved,
        in_specs=(block, P(), P(), P(), P(), P()),
        out_specs=block,
        check_vma=False,
    )
```

```python
import functools

import jax
import jax.numpy as jnp
from jax import lax
from jax.experimental import pallas as pl
from jax.experimental.pallas import tpu as pltpu
from jax.sharding import PartitionSpec as P

LANES = 128
BF16 = jnp.bfloat16
F32 = jnp.float32
VMEM_LIMIT = 16 * 1024 * 1024


def sigmoid(x):
    return 0.5 * jnp.tanh(0.5 * x) + 0.5


def norm_rows(x, gain):
    center = x - jnp.mean(x, axis=-1, keepdims=True)
    spread = jnp.mean(center * center, axis=-1, keepdims=True)
    return (center * lax.rsqrt(spread + 1e-05) * gain).astype(BF16)


def block_rows(first, second):
    split = LANES // first
    n1 = second // split
    return [l * n1 + s for s in range(n1) for l in range(split)]


def load_block(padded, first, second):
    rows = block_rows(first, second)
    return jnp.concatenate([padded[pl.ds(row, first, stride=second + 1), :] for row in rows], axis=0)


def block_copies(hbm, padded, sem):
    first, second, _ = hbm.shape
    return [(hbm.at[f], padded.at[pl.ds(f * (second + 1), second), :], sem) for f in range(first)]


def wait_block(hbm, padded, sem):
    first, second, chans = hbm.shape
    whole = padded.at[pl.ds(0, first * second), :]
    pltpu.make_async_copy(whole, whole, sem).wait()


def branch_planes(normed, w_t, n1, planes):
    hidden = w_t.shape[0] // 4
    pad = n1 + 1
    proj = lax.dot_general(w_t, normed, (((1,), (1,)), ((), ())), preferred_element_type=F32)
    for side in range(2):
        at = 2 * side * hidden
        value = sigmoid(proj[at : at + hidden]) * proj[at + hidden : at + 2 * hidden]
        for s in range(n1):
            planes[pl.ds(side * hidden * pad + s, hidden, stride=pad), :] = value[:, s * LANES : (s + 1) * LANES]


def plane(planes, n1, channel):
    at = channel * (n1 + 1)
    return planes[at : at + n1, :].astype(BF16)


def leave_blocks(b_ref, keep_hbm, swap_hbm, sem):
    my_row, my_rest = lax.axis_index("row"), lax.axis_index("rest")
    for core, hbm in ((1, swap_hbm), (0, keep_hbm)):
        for r in range(hbm.shape[0]):
            for c in range(hbm.shape[1]):
                block = b_ref.at[jnp.bitwise_xor(my_row, r), jnp.bitwise_xor(my_rest, 2 * c + core)]
                pltpu.make_async_copy(block, hbm.at[r, c], sem).start()
    return pltpu.make_async_copy(b_ref, b_ref, sem)


def project_kernel(shared, pair_hbm, gain_hbm, w_hbm, send_hbm, *refs):
    if shared:
        keep_hbm, swap_hbm, padded, gain_ref, w_ref, planes, send_ref, b_ref, in_sems, out_sems = refs
    else:
        padded, gain_ref, w_ref, planes, send_ref, in_sems, out_sems = refs
    first, second, _ = pair_hbm.shape
    ndev, _, depth, n1, _ = send_ref.shape
    hidden = ndev * (depth + shared)
    copies = [pltpu.make_async_copy(*c) for c in block_copies(pair_hbm, padded, in_sems.at[0])]
    small = [
        pltpu.make_async_copy(gain_hbm, gain_ref, in_sems.at[1]),
        pltpu.make_async_copy(w_hbm.at[0], w_ref, in_sems.at[2]),
    ]
    for copy in small + copies:
        copy.start()
    for copy in small:
        copy.wait()
    wait_block(pair_hbm, padded, in_sems.at[0])
    normed = norm_rows(load_block(padded, first, second), gain_ref[0:1, :])
    branch_planes(normed, w_ref[...].T, n1, planes)
    sent = []

    def leave(vmem, hbm, sem):
        sent.append(pltpu.make_async_copy(vmem, hbm, sem))
        sent[-1].start()

    if shared:
        rows, rest = b_ref.shape[:2]
        for r in range(rows):
            for c in range(rest):
                at = ndev * depth + (r * rest + c) * 2 * shared
                for side in range(2):
                    for h in range(2 * shared):
                        b_ref[r, c, 2 * shared * side + h] = plane(planes, n1, side * hidden + at + h)
        sent.append(leave_blocks(b_ref, keep_hbm, swap_hbm, out_sems.at[2]))
    for part in range(2):
        own = range(part * ndev // 2, (part + 1) * ndev // 2)
        for device in own:
            for side in range(2):
                for h in range(depth):
                    send_ref[device, side, h] = plane(planes, n1, side * hidden + device * depth + h)
        at = pl.ds(own[0], len(own))
        leave(send_ref.at[at], send_hbm.at[at], out_sems.at[part])
    for copy in sent:
        copy.wait()


def move(copies):
    for copy in copies:
        copy.start()
    for copy in copies:
        copy.wait()


def prepare_kernel(
    pair_hbm, gain_ref, w_gate_ref, w_ref, out_gain_ref,
    ordered_hbm, gate_hbm, w_t_ref, gain_cols_ref, padded, ordered_ref, gate_ref, sems,
):
    first, second, _ = pair_hbm.shape
    for copy in block_copies(pair_hbm, padded, sems.at[0]):
        pltpu.make_async_copy(*copy).start()
    w_t_ref[...] = w_ref[1].T
    for u in range(2):
        wide = (LANES, out_gain_ref.shape[1])
        gain_cols_ref[u] = jnp.broadcast_to(out_gain_ref[u : u + 1, :], wide).T
    wait_block(pair_hbm, padded, sems.at[0])
    x = load_block(padded, first, second)
    ordered_ref[...] = x
    normed = norm_rows(x, gain_ref[0:1, :])
    gate_ref[...] = sigmoid(jnp.dot(normed, w_gate_ref[0], preferred_element_type=F32))
    move([
        pltpu.make_async_copy(ordered_ref, ordered_hbm, sems.at[1]),
        pltpu.make_async_copy(gate_ref, gate_hbm, sems.at[2]),
    ])


def gate_kernel(first_hbm, gain_ref, w_gate_ref, gate_hbm, first_ref, gate_ref, sems):
    move([pltpu.make_async_copy(first_hbm, first_ref, sems.at[0])])
    normed = norm_rows(first_ref[...], gain_ref[1:2, :])
    gate_ref[...] = sigmoid(jnp.dot(normed, w_gate_ref[1], preferred_element_type=F32))
    move([pltpu.make_async_copy(gate_ref, gate_hbm, sems.at[1])])


def stage(part_refs, b_ref):
    rows = b_ref.shape[1]
    for r in range(rows):
        b_ref[0, r] = part_refs[r][...]
    for apart, part_ref in enumerate(part_refs[rows:], 1):
        b_ref[apart] = part_ref[...]


def dense_half(b_ref, i, first, dense):
    highs, rows, _, _, n1, _ = b_ref.shape
    split = LANES // first
    my_row, my_rest = lax.axis_index("row"), lax.axis_index("rest")
    for c in range(2 * highs):
        apart = jnp.bitwise_xor(my_rest, c)
        for l in range(split):
            at = (c * split + l) * n1
            dense[at : at + n1, :] = jnp.concatenate(
                [
                    b_ref[apart // 2, jnp.bitwise_xor(my_row, r), apart % 2, i, :, l * first : (l + 1) * first]
                    for r in range(rows)
                ],
                axis=1,
            )


def transposed_product(left, right):
    return lax.dot_general(
        right[...], left[...], (((0,), (0,)), ((), ())), preferred_element_type=F32
    ).astype(BF16)


def outgoing_half_kernel(cols, first, *refs):
    *part_refs, out_ref, left, right, b_ref = refs
    rows, depth = out_ref.shape[0] // cols, out_ref.shape[1]
    places = [[slot(cols, r, c) for c in range(cols)] for r in range(rows)]
    stage(part_refs, b_ref)
    for h in range(depth):
        dense_half(b_ref, h, first, left)
        dense_half(b_ref, depth + h, first, right)
        scatter_product(transposed_product(left, right), first, h, places, out_ref)


def outgoing_kernel(cols, first, recv_ref, *refs):
    *half_ref, out_ref, left, right = refs
    ndev, _, depth, n1, _ = recv_ref.shape
    split = LANES // first
    rows = ndev // cols
    places = [[slot(cols, r, c) for c in range(cols)] for r in range(rows)]
    for h in range(depth):
        for side, dense in ((0, left), (1, right)):
            for c in range(cols):
                for l in range(split):
                    at = (c * split + l) * n1
                    dense[at : at + n1, :] = jnp.concatenate(
                        [
                            recv_ref[places[r][c], side, h, :, l * first : (l + 1) * first]
                            for r in range(rows)
                        ],
                        axis=1,
                    )
        scatter_product(transposed_product(left, right), first, h, places, out_ref)
    for ref in half_ref:
        out_ref[:, depth:] = ref[...]


def slot(cols, r, c):
    rest = cols // 2
    return (r * rest + c % rest) * 2 + c // rest


def scatter_product(summed, first, h, places, out_ref):
    split = LANES // first
    n1 = out_ref.shape[2]
    for r, row in enumerate(places):
        for c, place in enumerate(row):
            out_ref[place, h] = jnp.concatenate(
                [
                    summed[(c * split + l) * n1 : (c * split + l + 1) * n1, r * first : (r + 1) * first]
                    for l in range(split)
                ],
                axis=1,
            )


def incoming_layout_kernel(first, *refs):
    *part_refs, dense_ref, b_ref = refs
    stage(part_refs, b_ref)
    for h in range(dense_ref.shape[0]):
        dense_half(b_ref, h, first, dense_ref.at[h])


def incoming_kernel(cols, first, recv_ref, dense_ref, out_ref, left):
    ndev, depth, n1, _ = recv_ref.shape
    split = LANES // first
    rows = ndev // cols
    places = [[c * rows + r for c in range(cols // 2)] for r in range(rows)]
    for h in range(depth):
        for c in range(cols):
            for l in range(split):
                at = (c * split + l) * n1
                left[at : at + n1, :] = jnp.concatenate(
                    [recv_ref[slot(cols, r, c), h, :, l * first : (l + 1) * first] for r in range(rows)], axis=1
                )
        summed = lax.dot_general(
            dense_ref[h], left[...], (((1,), (1,)), ((), ())), preferred_element_type=F32
        ).astype(BF16)
        scatter_product(summed, first, h, places, out_ref)


def output(x, gain_cols, w, normal):
    hidden, n1, _ = x.shape
    pad = n1 + 1
    center = x - jnp.mean(x, axis=0, keepdims=True)
    spread = jnp.mean(center * center, axis=0, keepdims=True)
    scaled = center * lax.rsqrt(spread + 1e-05)
    for h in range(hidden):
        normal[h * pad : h * pad + n1, :] = scaled[h]
    mixed = jnp.concatenate([normal[pl.ds(s, hidden, stride=pad), :] * gain_cols for s in range(n1)], axis=1)
    high = mixed.astype(BF16)
    low = (mixed - high.astype(F32)).astype(BF16)
    return lax.dot_general(
        jnp.concatenate([high, low], axis=0),
        jnp.concatenate([w, w], axis=0),
        (((0,), (0,)), ((), ())),
        preferred_element_type=F32,
    )


def middle_kernel(
    ordered_ref, summed_ref, gate_ref, gain_cols_ref, w_out_ref, gain_ref, w_t_ref,
    first_hbm, send_hbm, keep_hbm, swap_hbm, normal, planes, first_ref, send_ref, b_ref, sems,
):
    rows, rest, depth, n1, _ = send_ref.shape
    halves = send_hbm.shape[2]
    hidden = rows * rest * depth
    copies = []

    def leave(vmem, hbm):
        copies.append(pltpu.make_async_copy(vmem, hbm, sems.at[len(copies)]))
        copies[-1].start()

    shared = summed_ref.shape[3] - depth // 2
    own = summed_ref.shape[3] - 2 * shared
    x = summed_ref[:, :, :, :own].astype(F32).reshape(-1, n1, LANES)
    if shared:
        x_shared = summed_ref[:, :, 0, own:].astype(F32) + summed_ref[:, :, 1, own:].astype(F32)
        x = jnp.concatenate([x, x_shared.reshape(-1, n1, LANES)], axis=0)
    z = ordered_ref[...] + gate_ref[...] * output(x, gain_cols_ref[0], w_out_ref[0], normal)
    first_ref[...] = z
    leave(first_ref, first_hbm)
    branch_planes(norm_rows(z, gain_ref[1:2, :]), w_t_ref[...], n1, planes)
    for r in range(rows):
        for c in range(rest):
            for h in range(depth):
                b_ref[r, c, h] = plane(planes, n1, hidden + (c * rows + r) * depth + h)
    copies.append(leave_blocks(b_ref, keep_hbm, swap_hbm, sems.at[len(copies)]))
    for r in range(rows):
        for c in range(rest):
            for h in range(depth):
                send_ref[r, c, h] = plane(planes, n1, (c * rows + r) * depth + h)
        if r % (rows // 2) == rows // 2 - 1:
            own = pl.ds(r + 1 - rows // 2, rows // 2)
            for half in range(halves):
                leave(send_ref.at[own], send_hbm.at[own, :, half])
    for copy in copies:
        copy.wait()


def last_kernel(
    first_ref, summed_ref, gate_ref, gain_cols_ref, w_out_ref, updated_hbm, normal, padded, sems
):
    first, second, _ = updated_hbm.shape
    z = first_ref[...] + gate_ref[...] * output(summed_ref[...].astype(F32), gain_cols_ref[1], w_out_ref[1], normal)
    for i, row in enumerate(block_rows(first, second)):
        padded[pl.ds(row, first, stride=second + 1), :] = z[i * first : (i + 1) * first]
    copies = [
        pltpu.make_async_copy(vmem, hbm, sem) for hbm, vmem, sem in block_copies(updated_hbm, padded, sems.at[0])
    ]
    for copy in copies:
        copy.start()
    wait_block(updated_hbm, padded, sems.at[0])


def call(kernel, outs, scratch, flops, *args, pinned=None, spaces=None):
    moved = sum(a.size * a.dtype.itemsize for a in args) + sum(o.size * o.dtype.itemsize for o in outs)
    pinned = pinned or [None] * len(args)
    spaces = spaces or [None] * len(outs)
    args = [a if space is None else pltpu.with_memory_space_constraint(a, space) for a, space in zip(args, pinned)]
    outs = [o if space is None else space(o.shape, o.dtype) for o, space in zip(outs, spaces)]
    in_specs = [pl.BlockSpec(memory_space=space or pltpu.VMEM) for space in pinned]
    out_specs = [pl.BlockSpec(memory_space=space or pltpu.VMEM) for space in spaces]
    return pl.pallas_call(
        kernel,
        out_shape=outs,
        in_specs=in_specs,
        out_specs=out_specs,
        scratch_shapes=scratch,
        compiler_params=pltpu.CompilerParams(vmem_limit_bytes=VMEM_LIMIT),
        cost_estimate=pl.CostEstimate(flops=flops, bytes_accessed=moved, transcendentals=0),
    )(*args)


def spread(keep, swap):
    rows, highs = keep.shape[:2]
    rest = 2 * highs

    def swapped(x, axis, size, apart):
        return lax.ppermute(x, axis, [(d, d ^ apart) for d in range(size)]) if apart else x

    b = jnp.stack([keep, swapped(swap, "rest", rest, 1)], axis=2)
    far = [
        swapped(jnp.stack([swapped(b[r, c], "row", rows, r) for r in range(rows)]), "rest", rest, 2 * c)
        for c in range(1, highs)
    ]
    return [swapped(b[r, 0], "row", rows, r) for r in range(rows)] + far


def body(rows, cols, pair, norm_in_gain, w_proj, w_gate, norm_out_gain, w_out):
    first, second, chans = pair.shape
    hidden = w_out.shape[1]
    ndev = rows * cols
    rest = cols // 2
    shared = hidden // ndev // 4
    depth, half_depth = hidden // ndev - shared, 2 * hidden // ndev
    count = first * second
    n1 = count // LANES
    total = rows * first

    flat_shape = jax.ShapeDtypeStruct((count, chans), F32)
    planes = pltpu.VMEM(((2 * hidden + 1) * (n1 + 1), LANES), F32)
    normal = pltpu.VMEM(((hidden + 1) * (n1 + 1), LANES), F32)
    padded = pltpu.VMEM(((first + 1) * (second + 1), chans), F32)
    proj_flops = 2 * count * chans * 4 * hidden
    gate_flops = 2 * count * chans * chans
    tri_flops = 2 * (depth + shared) * total**3

    def shaped(*shape):
        return jax.ShapeDtypeStruct(shape + (n1, LANES), BF16)

    out_shapes = [shaped(ndev, 2, depth)] + [shaped(rows, rest // 2, 4 * shared)] * (2 if shared else 0)
    send, *swaps = call(
        functools.partial(project_kernel, shared),
        out_shapes,
        [
            padded,
            pltpu.VMEM(norm_in_gain.shape, F32),
            pltpu.VMEM(w_proj.shape[1:], BF16),
            planes,
            pltpu.VMEM(out_shapes[0].shape, BF16),
        ]
        + ([pltpu.VMEM((rows, rest, 4 * shared, n1, LANES), BF16)] if shared else [])
        + [pltpu.SemaphoreType.DMA((3,)), pltpu.SemaphoreType.DMA((3,))],
        proj_flops, pair, norm_in_gain, w_proj,
        pinned=[pltpu.HBM] * 3, spaces=[pltpu.HBM] * len(out_shapes),
    )
    recv = lax.all_to_all(send, ("row", "rest", "half"), 0, 0, tiled=True)
    prepared = call(
        prepare_kernel,
        [
            flat_shape,
            flat_shape,
            jax.ShapeDtypeStruct((4 * hidden, chans), BF16),
            jax.ShapeDtypeStruct((2, hidden, LANES), F32),
        ],
        [padded, pltpu.VMEM(flat_shape.shape, F32), pltpu.VMEM(flat_shape.shape, F32), pltpu.SemaphoreType.DMA((3,))],
        gate_flops,
        pair, norm_in_gain, w_gate, w_proj, norm_out_gain,
        pinned=[pltpu.HBM] + [None] * 4, spaces=[pltpu.HBM, pltpu.HBM, None, None],
    )
    halves = []
    if shared:
        halves = call(
            functools.partial(outgoing_half_kernel, cols, first),
            [shaped(ndev, 2 * shared)],
            [
                pltpu.VMEM((rest * second, total), BF16),
                pltpu.VMEM((rest * second, total), BF16),
                pltpu.VMEM((rest // 2, rows, 2, 4 * shared, n1, LANES), BF16),
            ],
            tri_flops // 4, *spread(*swaps),
        )
    recv, halves, (ordered, gate, w_t, gain_cols) = lax.optimization_barrier((recv, halves, prepared))
    (product,) = call(
        functools.partial(outgoing_kernel, cols, first),
        [shaped(ndev, depth + 2 * shared)],
        [pltpu.VMEM((cols * second, total), BF16)] * 2,
        tri_flops, recv, *halves,
    )
    summed = lax.all_to_all(product, ("row", "rest", "half"), 0, 0, tiled=True)
    send_shape, b_shape = shaped(rows, rest, 2, half_depth), shaped(rows, rest // 2, half_depth)
    middle, send, keep, swap = call(
        middle_kernel,
        [flat_shape, send_shape, b_shape, b_shape],
        [
            normal,
            planes,
            pltpu.VMEM(flat_shape.shape, F32),
            pltpu.VMEM((rows, rest, half_depth, n1, LANES), BF16),
            pltpu.VMEM((rows, rest, half_depth, n1, LANES), BF16),
            pltpu.SemaphoreType.DMA((6,)),
        ],
        proj_flops + gate_flops,
        ordered, summed.reshape(rows, rest, 2, depth + 2 * shared, n1, LANES), gate, gain_cols, w_out, norm_in_gain, w_t,
        spaces=[pltpu.HBM] * 4,
    )
    recv = lax.all_to_all(
        send.reshape(ndev, half_depth, n1, LANES), ("row", "rest", "half"), 0, 0, tiled=True
    )
    (gate,) = call(
        gate_kernel, [flat_shape],
        [pltpu.VMEM(flat_shape.shape, F32), pltpu.VMEM(flat_shape.shape, F32), pltpu.SemaphoreType.DMA((2,))],
        gate_flops, middle, norm_in_gain, w_gate,
        pinned=[pltpu.HBM, None, None], spaces=[pltpu.HBM],
    )
    dense = call(
        functools.partial(incoming_layout_kernel, first),
        [jax.ShapeDtypeStruct((half_depth, rest * second, total), BF16)],
        [pltpu.VMEM((rest // 2, rows, 2, half_depth, n1, LANES), BF16)],
        0, *spread(keep, swap),
    )
    recv, gate, dense = lax.optimization_barrier((recv, gate, dense))
    (product,) = call(
        functools.partial(incoming_kernel, cols, first),
        [shaped(rows * rest, half_depth)], [pltpu.VMEM((cols * second, total), BF16)],
        tri_flops, recv, *dense,
    )
    summed = lax.all_to_all(product, ("rest", "row"), 0, 0, tiled=True)
    (updated,) = call(
        last_kernel,
        [jax.ShapeDtypeStruct(pair.shape, F32)], [normal, padded, pltpu.SemaphoreType.DMA((1,))], gate_flops,
        middle, summed.reshape(hidden, n1, LANES), gate, gain_cols, w_out, spaces=[pltpu.HBM],
    )
    return updated


def solution(mesh):
    rows, cols = mesh.shape["row"], mesh.shape["col"]
    halved = jax.sharding.Mesh(mesh.devices.reshape(rows, 2, cols // 2), ("row", "half", "rest"))
    block = P("row", ("half", "rest"), None)
    return jax.shard_map(
        functools.partial(body, rows, cols),
        mesh=halved,
        in_specs=(block, P(), P(), P(), P(), P()),
        out_specs=block,
        check_vma=False,
    )
```
